512 devices in a mesh: dap: 128 (over z_lo, y, x, core), dp: 4 (over z_hi).
Axes of the slice: x: 4, y: 8, z: 8 (z_hi: 4, z_lo: 2; z = z_hi * 2 + z_lo), core: 2. Of those that a mesh axis runs over, the one named last changes fastest.
Arguments:
- pair: bfloat16 [1024, 256, 128], P(('dp', 'dap')), parts along dimension 0, may hold values from -6 to 6
- pair_mask: int32 [1024, 256], P(('dp', 'dap')), parts along dimension 0, may hold values from 0 to 1, as said below
- w_left: bfloat16 [128, 256], replicated, may hold values from -0.5 to 0.5
- w_right: bfloat16 [128, 256], replicated, may hold values from -0.5 to 0.5
- w_tri_gate: bfloat16 [128, 128], replicated, may hold values from -0.5 to 0.5
- w_tri_out: bfloat16 [128, 128], replicated, may hold values from -0.5 to 0.5
- w_attend: bfloat16 [128, 512], replicated, may hold values from -0.5 to 0.5
- w_bias: bfloat16 [128, 4], replicated
- w_att_out: bfloat16 [128, 128], replicated, may hold values from -0.5 to 0.5
Outputs:
- pair_out: float32 [1024, 256, 128], P('dp', 'dap'), parts along dimension 0
The draws below stay inside these ranges and needn't reach their ends.
There are 4 independent parts, one for each index of `dp`. The reference program is written for one: setup_inputs(seed, part) draws one part's arguments, and reference() takes and returns one part's arrays. A program takes and returns all parts, laid end to end along the dimension named above; an argument that names none is the same for every part. Nothing has to cross between parts.
Inputs may be any that keep to these rules, and one draw needn't show every extreme that they name: pair_mask[i, i] = 1 for every residue i.
All inputs are finite; a program needn't handle non-finite values.
Results may differ from the reference program's by a relative error of at most 0.014.
The reference program's roundings to bfloat16 on the way (of `zn`, `left_edge`, `right_edge`, `tn`, `yn`, `bias`, `weights` and `att`) count: a program that leaves them out, or rounds other values in their place, can miss the bound.
Values may be sent and summed in bfloat16 or wider, within the bound.
A program may use at most 128 MiB of HBM per device.

```python
import jax
import jax.numpy as jnp
from jax import lax

C = 128
H = 128
HEADS = 4
HEAD_DIM = 32
N = 256


def draw_pair_mask(key, part):
    levels = jax.random.randint(key, (N, N), 0, 8)
    index = jnp.arange(N)
    diagonal = index[:, None] == index[None, :]
    return jnp.where(diagonal, 1, (levels > 0).astype(jnp.int32)).astype(jnp.int32)


def draw_w_bias(key, part):
    base = jax.random.normal(key, (C, HEADS), jnp.float32) / jnp.sqrt(jnp.float32(C))
    return base.astype(jnp.bfloat16)


def shard_levels(key, shape, pieces, smallest, high):
    def one(axis_at, shards_of):
        draws = jax.random.uniform(jax.random.fold_in(jax.random.fold_in(key, 6), axis_at), (shards_of,), jnp.float32, smallest / len(pieces), high / len(pieces))
        return jnp.repeat(jnp.exp(draws), shape[axis_at] // shards_of).reshape((-1,) + (1,) * (len(shape) - axis_at - 1))

    level = one(*pieces[0])
    for cut in pieces[1:]:
        level = level * one(*cut)
    return level


def scatter_about(rng, dims, scale, limit, shards=(), kind=jnp.bfloat16):
    array = jax.random.normal(rng, dims, jnp.float32) * scale
    if len(shards) > 0:
        array = shard_levels(rng, dims, shards, -0.22, 0.18) * array
    return jnp.clip(array, min=-limit, max=limit).astype(kind)


def setup_inputs(seed: int = 0, part: int = 0) -> dict:
    streams_of = jax.random.split(jax.random.key(seed), 10)
    part_splits = jax.random.split(jax.random.fold_in(streams_of[9], part), 10)
    return {
        "pair": scatter_about(part_splits[0], (N, N, C), 1.0, 6.0, ((0, 128),)),
        "pair_mask": draw_pair_mask(jax.random.fold_in(jax.random.fold_in(streams_of[9], part), 71), part),
        "w_left": scatter_about(streams_of[2], (C, 2 * H), C ** -0.5, 0.5),
        "w_right": scatter_about(streams_of[3], (C, 2 * H), C ** -0.5, 0.5),
        "w_tri_gate": scatter_about(streams_of[4], (C, C), C ** -0.5, 0.5),
        "w_tri_out": scatter_about(streams_of[5], (H, C), H ** -0.5, 0.5),
        "w_attend": scatter_about(streams_of[6], (C, 4 * HEADS * HEAD_DIM), C ** -0.5, 0.5),
        "w_bias": draw_w_bias(jax.random.fold_in(streams_of[9], 71), part),
        "w_att_out": scatter_about(streams_of[8], (HEADS * HEAD_DIM, C), (HEADS * HEAD_DIM) ** -0.5, 0.5),
    }


def layer_norm(x):
    x = x.astype(jnp.float32)
    mean = lax.optimization_barrier(jnp.mean(x, axis=-1, keepdims=True))
    var = lax.optimization_barrier(jnp.mean((x - mean) * (x - mean), axis=-1, keepdims=True))
    return (x - mean) / jnp.sqrt(var + 1e-05)

def matmul(x, w):
    flat = x.reshape(-1, x.shape[-1])
    return jnp.dot(flat, w, preferred_element_type=jnp.float32).reshape(x.shape[:-1] + (w.shape[1],))

def reference(pair, pair_mask, w_left, w_right, w_tri_gate, w_tri_out, w_attend, w_bias, w_att_out):
    hidden = w_tri_out.shape[0]
    inner = w_att_out.shape[0]
    heads = w_bias.shape[1]
    head_dim = inner // heads
    rows = pair.shape[0]
    maskf = pair_mask.astype(jnp.float32)
    zn = layer_norm(pair).astype(jnp.bfloat16)
    left = matmul(zn, w_left)
    left_edge = (jax.nn.sigmoid(left[..., :hidden]) * left[..., hidden:] * maskf[..., None]).astype(jnp.bfloat16)
    right = matmul(zn, w_right)
    right_edge = (jax.nn.sigmoid(right[..., :hidden]) * right[..., hidden:] * maskf[..., None]).astype(jnp.bfloat16)
    tri = jnp.einsum('ikc,jkc->ijc', left_edge.astype(jnp.float32), right_edge.astype(jnp.float32))
    tn = layer_norm(tri).astype(jnp.bfloat16)
    update = jax.nn.sigmoid(matmul(zn, w_tri_gate)) * matmul(tn, w_tri_out)
    pair1 = pair.astype(jnp.float32) + update
    yn = layer_norm(pair1).astype(jnp.bfloat16)
    proj = matmul(yn, w_attend)
    query = proj[..., :inner].astype(jnp.bfloat16).reshape(rows, rows, heads, head_dim)
    keys = proj[..., inner:2 * inner].astype(jnp.bfloat16).reshape(rows, rows, heads, head_dim)
    values = proj[..., 2 * inner:3 * inner].astype(jnp.bfloat16).reshape(rows, rows, heads, head_dim)
    gate = jax.nn.sigmoid(proj[..., 3 * inner:])
    bias = jnp.einsum('kic,ch->hki', yn.astype(jnp.float32), w_bias.astype(jnp.float32)).astype(jnp.bfloat16)
    scores = jnp.einsum('ijhd,kjhd->jhki', query.astype(jnp.float32), keys.astype(jnp.float32)) / jnp.sqrt(jnp.float32(head_dim))
    scores = scores + bias.astype(jnp.float32)[None]
    live = jnp.transpose(maskf)[:, None, :, None]
    scores = jnp.where(live > 0.5, scores, jnp.float32(-1000000000.0))
    weights = jax.nn.softmax(scores, axis=2).astype(jnp.bfloat16)
    summed = jnp.einsum('jhki,kjhd->ijhd', weights.astype(jnp.float32), values.astype(jnp.float32)).reshape(rows, rows, inner)
    att = (gate * summed).astype(jnp.bfloat16)
    return pair1 + matmul(att, w_att_out)
```

```python
import functools

import jax
import jax.numpy as jnp
from jax import lax
from jax.experimental import pallas as pl
from jax.experimental.pallas import tpu as pltpu
from jax.sharding import PartitionSpec as P

MESH = pl.DeviceIdType.MESH
BF16 = jnp.bfloat16
F32 = jnp.float32
NY = 8
NQ = 16
YN = (((0,), (0,)), ((), ()))
NT = (((1,), (1,)), ((), ()))
TT = (((0,), (1,)), ((), ()))


def device_of(q, y):
    return (q // 8) * 64 + y * 8 + q % 8


def mm(a, b, dims=(((1,), (0,)), ((), ()))):
    return lax.dot_general(a, b, dims, preferred_element_type=F32)


def norm(x, axis):
    mean = jnp.mean(x, axis=axis, keepdims=True)
    d = x - mean
    var = jnp.mean(d * d, axis=axis, keepdims=True)
    return d * lax.rsqrt(var + 1e-05)


def grid_of(n, m):
    return (
        lax.broadcasted_iota(jnp.int32, (n, m), 0),
        lax.broadcasted_iota(jnp.int32, (n, m), 1),
    )


def onehot(cond):
    return jnp.where(cond, F32(1), F32(0)).astype(BF16)


def kernel(
    pair_ref, mask_ref, wl_ref, wr_ref, wg_ref, wo_ref, wa_ref, wb_ref, wao_ref, out_ref,
    send_l, send_r, send_m, got_l, got_r, got_p, got_m,
    next_l, next_r, next_p, have_l, have_r, have_p,
    send_t, got_t, next_t, have_t,
    send_b, got_b, next_b, have_b, scores, ssem, rsem,
):
    me = lax.axis_index("dap")
    zl, y, xc = me // 64, (me // 8) % 8, me % 8
    q = zl * 8 + xc

    barrier = pltpu.get_barrier_semaphore()

    def greet_y(s, c):
        pl.semaphore_signal(barrier, inc=1, device_id={"dap": device_of(q, (y + s) % NY)}, device_id_type=MESH)
        return c

    def greet_q(s, c):
        pl.semaphore_signal(barrier, inc=1, device_id={"dap": device_of((q + s) % NQ, y)}, device_id_type=MESH)
        return c

    lax.fori_loop(1, NY, greet_y, 0)
    lax.fori_loop(1, NQ, greet_q, 0)

    def send_y(src, dst, k):
        def step(s, c):
            to = (y + s) % NY
            pltpu.make_async_remote_copy(
                src_ref=src(to), dst_ref=dst.at[y], send_sem=ssem.at[k], recv_sem=rsem.at[k],
                device_id={"dap": device_of(q, to)}, device_id_type=MESH,
            ).start()
            return c

        lax.fori_loop(1, NY, step, 0)

    def send_q(src, dst, k):
        def step(s, c):
            to = (q + s) % NQ
            pltpu.make_async_remote_copy(
                src_ref=src(to), dst_ref=dst(), send_sem=ssem.at[k], recv_sem=rsem.at[k],
                device_id={"dap": device_of(to, y)}, device_id_type=MESH,
            ).start()
            return c

        lax.fori_loop(1, NQ, step, 0)

    def wait_on(ref, sem):
        pltpu.make_async_copy(ref, ref, sem).wait()

    x = pair_ref[...].astype(F32).reshape(512, 128)
    zn = norm(x, 1).astype(BF16)
    maskf = mask_ref[...].astype(F32)
    mask_row = jnp.concatenate([maskf[0:1], maskf[1:2]], axis=1)

    def edge(w_ref):
        both = mm(w_ref[...], zn, TT)
        return (jax.nn.sigmoid(both[:128]) * both[128:] * mask_row).astype(BF16)

    def put_edge(ref, value):
        for ii in range(2):
            ref[:, ii] = value[:, ii * 256 : (ii + 1) * 256].reshape(NY, 16, 256)

    put_edge(send_l, edge(wl_ref))
    pl.semaphore_wait(barrier, NY + NQ - 2)
    send_y(lambda to: send_l.at[to], got_l, 0)
    put_edge(send_r, edge(wr_ref))
    send_y(lambda to: send_r.at[to], got_r, 1)

    lane, col = grid_of(128, 128)
    rows0 = jnp.where(lane % 2 == 0, maskf[0:1, :128], maskf[0:1, 128:])
    rows1 = jnp.where(lane % 2 == 0, maskf[1:2, :128], maskf[1:2, 128:])
    eye = onehot(lane == col)
    spread = jnp.where(lane < 64, rows0, rows1).astype(BF16)
    send_m[...] = mm(eye, spread, NT).astype(BF16).reshape(NY, 16, 128)
    send_y(lambda to: pair_ref.at[:, :, to], got_p, 2)
    send_y(lambda to: send_m.at[to], got_m, 3)
    got_l[y] = send_l[y]
    got_r[y] = send_r[y]
    got_p[y] = pair_ref[:, :, y]
    got_m[y] = send_m[y]

    r, s = grid_of(256, 256)
    turn = onehot((r // 16 == s % 16) & ((r // 8) % 2 == (s // 16) % 2) & (r % 8 == s // 32))
    back = onehot((s // 16 == r % 16) & ((s // 8) % 2 == (r // 16) % 2) & (s % 8 == r // 32))

    wait_on(got_l.at[pl.ds(0, NY - 1)], rsem.at[0])
    next_l[...] = mm(turn, got_l[...].reshape(256, 256)).astype(BF16).reshape(NQ, 16, 256)
    send_q(lambda to: next_l.at[to], lambda: have_l.at[q], 4)
    wait_on(got_r.at[pl.ds(0, NY - 1)], rsem.at[1])
    next_r[...] = mm(turn, got_r[...].reshape(256, 256)).astype(BF16).reshape(NQ, 16, 256)
    send_q(lambda to: next_r.at[to], lambda: have_r.at[q], 5)
    have_l[q] = next_l[q]
    have_r[q] = next_r[q]

    wait_on(got_p.at[pl.ds(0, NY - 1)], rsem.at[2])
    wait_on(got_m.at[pl.ds(0, NY - 1)], rsem.at[3])
    m0 = got_m[...].astype(F32)
    m1 = pltpu.roll(m0.reshape(128, 128), 64, 1).reshape(NY, 16, 128)
    m01 = jnp.stack([m0, m1], axis=1).reshape(256, 128).astype(BF16)
    m01 = mm(turn, m01).astype(BF16).reshape(8, 2, 16, 128)
    for z in range(2):
        part = mm(turn, got_p[:, :, z].reshape(256, 128)).astype(BF16)
        next_p[z * 8 : z * 8 + 8, 0:2] = part.reshape(8, 2, 16, 128)
        next_p[z * 8 : z * 8 + 8, 2:4] = m01
    send_q(lambda to: next_p.at[to], lambda: have_p.at[q], 6)
    have_p[q] = next_p[q]

    wait_on(have_l.at[pl.ds(0, NQ - 1)], rsem.at[4])
    wait_on(have_r.at[pl.ds(0, NQ - 1)], rsem.at[5])
    tri = mm(have_r[...].reshape(256, 256), have_l[...].reshape(256, 256), NT)
    send_t[...] = tri.astype(BF16).reshape(NQ, 16, 256)
    send_q(lambda to: send_t.at[to], lambda: got_t.at[q], 7)
    got_t[q] = send_t[q]

    wait_on(have_p.at[pl.ds(0, NQ - 1)], rsem.at[6])
    pairs, gates, lives = [], [], []
    pick = onehot(lane == zl)
    for jj in range(2):
        p = have_p[:, jj].reshape(256, 128).astype(F32)
        zc = norm(p, 1).astype(BF16)
        pairs.append(p)
        gates.append(jax.nn.sigmoid(mm(zc, wg_ref[...])))
        lives.append(mm(have_p[:, 2 + jj].reshape(256, 128), pick))
    wa = wa_ref[...]
    wk = wa[:, 128:256]
    wq_t, wv_t, wgate_t = wa[:, :128], wa[:, 256:384], wa[:, 384:]

    wait_on(got_t.at[pl.ds(0, NQ - 1)], rsem.at[7])
    next_t[...] = mm(back, got_t[...].reshape(256, 256)).astype(BF16).reshape(NY, 32, 256)
    send_y(lambda to: next_t.at[to], have_t, 8)
    have_t[y] = next_t[y]
    order = onehot(
        (col // 16 == lane % 8)
        & ((col // 8) % 2 == lane // 64)
        & ((col // 4) % 2 == (lane // 8) % 2)
        & (col % 4 == (lane // 16) % 4)
    )
    wait_on(have_t.at[pl.ds(0, NY - 1)], rsem.at[8])

    pair1, yns = [], []
    for jj in range(2):
        t = have_t[:, jj * 16 : (jj + 1) * 16].reshape(128, 256).astype(F32)
        tn = norm(t, 0).astype(BF16)
        p1 = pairs[jj] + gates[jj] * mm(tn, wo_ref[...], YN)
        pair1.append(p1)
        yns.append(norm(p1, 1).astype(BF16))

    parts = [mm(wb_ref[...], yn, TT) for yn in yns]
    both = jnp.concatenate(parts, axis=0)
    send_b[...] = jnp.concatenate([both[:, :128], both[:, 128:]], axis=0).astype(BF16)
    send_y(lambda to: send_b, got_b, 9)
    got_b[y] = send_b[...]

    keys, queries, values, out_gates = [], [], [], []
    for jj in range(2):
        keys.append(mm(yns[jj], wk).astype(BF16))
        queries.append(mm(wq_t, yns[jj], TT).astype(BF16))
        values.append(mm(wv_t, yns[jj], TT).astype(BF16))
        out_gates.append(jax.nn.sigmoid(mm(wgate_t, yns[jj], TT)))

    wait_on(got_b.at[pl.ds(0, NY - 1)], rsem.at[9])
    next_b[...] = mm(order, got_b[...].reshape(128, 128)).astype(BF16).reshape(8, 16, 128)
    send_q(lambda to: next_b, lambda: have_b.at[q], 10)
    have_b[q] = next_b[...]

    head_row = lax.broadcasted_iota(jnp.int32, (128, 256), 0) // 32
    scale = F32(32.0**-0.5)
    for jj in range(2):
        for h in range(4):
            qh = jnp.where(head_row == h, queries[jj].astype(F32), F32(0)).astype(BF16)
            scores[jj, h] = mm(keys[jj], qh) * scale

    wait_on(have_b.at[pl.ds(0, NQ - 1)], rsem.at[10])
    atts = [[], []]
    for h in range(4):
        bias = jnp.concatenate(
            [mm(eye, have_b[:, kh * 4 + h].reshape(256, 128), NT) for kh in range(2)], axis=0
        )
        for jj in range(2):
            live = jnp.concatenate([lives[jj], lives[jj]], axis=1) > 0.5
            sc = jnp.where(live, scores[jj, h] + bias, F32(-1e9))
            e = jnp.exp(sc - jnp.max(sc, axis=0, keepdims=True))
            w = (e / jnp.sum(e, axis=0, keepdims=True)).astype(BF16)
            o = mm(values[jj][h * 32 : (h + 1) * 32], w)
            atts[jj].append(out_gates[jj][h * 32 : (h + 1) * 32] * o)
    for jj in range(2):
        att = jnp.concatenate(atts[jj], axis=0).astype(BF16)
        res = pair1[jj] + mm(att, wao_ref[...], YN)
        for qq in range(NQ):
            for ii in range(2):
                start = (qq // 8) * 256 + (qq % 8) * 4 + ii * 2 + jj
                out_ref[pl.ds(start, 8, stride=32), :] = res[qq * 16 + ii * 8 : qq * 16 + ii * 8 + 8]

    for k, ref in (
        (0, got_l), (1, got_r), (2, got_p), (3, got_m), (8, have_t), (9, got_b),
    ):
        wait_on(ref.at[pl.ds(0, NY - 1)], ssem.at[k])
    for k, ref in ((4, have_l), (5, have_r), (6, have_p), (7, got_t), (10, have_b)):
        wait_on(ref.at[pl.ds(0, NQ - 1)], ssem.at[k])


def shards(pair, pair_mask, *weights):
    vm = pl.BlockSpec(memory_space=pltpu.VMEM)
    out = pl.pallas_call(
        kernel,
        out_shape=jax.ShapeDtypeStruct((512, 128), F32),
        in_specs=[vm] * 9,
        out_specs=vm,
        scratch_shapes=[
            pltpu.VMEM((NY, 2, 16, 256), BF16),
            pltpu.VMEM((NY, 2, 16, 256), BF16),
            pltpu.VMEM((NY, 16, 128), BF16),
            pltpu.VMEM((NY, 2, 16, 256), BF16),
            pltpu.VMEM((NY, 2, 16, 256), BF16),
            pltpu.VMEM((NY, 2, 2, 16, 128), BF16),
            pltpu.VMEM((NY, 16, 128), BF16),
            pltpu.VMEM((NQ, 16, 256), BF16),
            pltpu.VMEM((NQ, 16, 256), BF16),
            pltpu.VMEM((NQ, 4, 16, 128), BF16),
            pltpu.VMEM((NQ, 16, 256), BF16),
            pltpu.VMEM((NQ, 16, 256), BF16),
            pltpu.VMEM((NQ, 4, 16, 128), BF16),
            pltpu.VMEM((NQ, 16, 256), BF16),
            pltpu.VMEM((NQ, 16, 256), BF16),
            pltpu.VMEM((NY, 32, 256), BF16),
            pltpu.VMEM((NY, 32, 256), BF16),
            pltpu.VMEM((16, 128), BF16),
            pltpu.VMEM((NY, 16, 128), BF16),
            pltpu.VMEM((8, 16, 128), BF16),
            pltpu.VMEM((NQ, 8, 16, 128), BF16),
            pltpu.VMEM((2, 4, 256, 256), F32),
            pltpu.SemaphoreType.DMA((11,)),
            pltpu.SemaphoreType.DMA((11,)),
        ],
        compiler_params=pltpu.CompilerParams(
            collective_id=0, has_side_effects=True, vmem_limit_bytes=32 * 1024 * 1024
        ),
    )(pair.reshape(2, 2, 8, 16, 128), pair_mask, *weights)
    return out.reshape(256, 2, 128)


def solution(mesh):
    rows = ("dp", "dap")
    return jax.shard_map(
        shards,
        mesh=mesh,
        in_specs=(P(rows, None, None), P(rows, None), P(), P(), P(), P(), P(), P(), P()),
        out_specs=P("dp", "dap", None),
        check_vma=False,
    )
```

```python
import functools

import jax
import jax.numpy as jnp
from jax import lax
from jax.experimental import pallas as pl
from jax.experimental.pallas import tpu as pltpu
from jax.sharding import PartitionSpec as P

MESH = pl.DeviceIdType.MESH
BF16 = jnp.bfloat16
F32 = jnp.float32
NY = 8
NQ = 16
YN = (((0,), (0,)), ((), ()))
NT = (((1,), (1,)), ((), ()))
TT = (((0,), (1,)), ((), ()))


FAR_Y = (4, 3, 5, 2, 6, 1, 7)
FAR_Q = tuple((dz, dx, dc) for dz, dx in ((1, 2), (1, 1), (1, 3), (0, 2), (0, 1), (0, 3), (1, 0)) for dc in (0, 1)) + ((0, 0, 1),)
FAR_CHIP = tuple(step for step in FAR_Q if step[2] == 0)


def device_of(q, y):
    return (q // 8) * 64 + y * 8 + q % 8


def moved(q, step):
    dz, dx, dc = step
    return ((q // 8 + dz) % 2) * 8 + ((q // 2 + dx) % 4) * 2 + (q + dc) % 2


def mm(a, b, dims=(((1,), (0,)), ((), ()))):
    return lax.dot_general(a, b, dims, preferred_element_type=F32)


def norm(x, axis):
    mean = jnp.mean(x, axis=axis, keepdims=True)
    d = x - mean
    var = jnp.mean(d * d, axis=axis, keepdims=True)
    return d * lax.rsqrt(var + 1e-05)


def grid_of(n, m):
    return (
        lax.broadcasted_iota(jnp.int32, (n, m), 0),
        lax.broadcasted_iota(jnp.int32, (n, m), 1),
    )


def onehot(cond):
    return jnp.where(cond, F32(1), F32(0)).astype(BF16)


def kernel(
    pair_in, mask_in, wl_in, wr_in, wg_in, wo_in, wa_in, wb_in, wao_in, out_ref,
    pair_ref, mask_ref, wl_ref, wr_ref, wg_ref, wo_ref, wa_ref, wb_ref, wao_ref,
    send_l, send_r, send_m, got_l, got_r, got_p, got_m,
    next_l, next_r, next_p, have_l, have_r, have_p,
    send_t, got_t, next_t, have_t,
    send_b, got_b, next_b, have_b, scores, ssem, rsem, lsem,
):
    me = lax.axis_index("dap")
    zl, y, xc = me // 64, (me // 8) % 8, me % 8
    q = zl * 8 + xc

    loads = [
        pltpu.make_async_copy(a, b, lsem.at[k])
        for k, (a, b) in enumerate((
            (pair_in, pair_ref), (wl_in, wl_ref), (mask_in, mask_ref), (wr_in, wr_ref), (wg_in, wg_ref),
            (wo_in, wo_ref), (wa_in, wa_ref), (wb_in, wb_ref), (wao_in, wao_ref),
        ))
    ]
    for load in loads:
        load.start()
    barrier = pltpu.get_barrier_semaphore()

    peers = [device_of(q, (y + s) % NY) for s in FAR_Y] + [device_of(moved(q, step), y) for step in FAR_Q]
    for peer in peers:
        pl.semaphore_signal(barrier, inc=1, device_id={"dap": peer}, device_id_type=MESH)

    sent, due = {}, {}

    def send(src, dst, k, peer):
        pltpu.make_async_remote_copy(
            src_ref=src, dst_ref=dst, send_sem=ssem.at[k], recv_sem=rsem.at[k],
            device_id={"dap": peer}, device_id_type=MESH,
        ).start()

    def send_y(src, dst, k):
        sent[k] = due[k] = dst.at[pl.ds(0, NY - 1)]
        for s in FAR_Y:
            to = (y + s) % NY
            send(src(to), dst.at[y], k, device_of(q, to))

    def send_q(src, dst, k):
        sent[k] = due[k] = dst.at[pl.ds(0, NQ - 1)]
        for step in FAR_Q:
            to = moved(q, step)
            send(src(to), dst.at[q], k, device_of(to, y))

    def wait_on(ref, sem):
        pltpu.make_async_copy(ref, ref, sem).wait()

    def arrive(k):
        wait_on(due.pop(k), rsem.at[k])

    for load in loads[:3]:
        load.wait()
    x = pair_ref[...].astype(F32).reshape(512, 128)
    zn = norm(x, 1).astype(BF16)
    maskf = mask_ref[...].astype(F32)
    mask_row = jnp.concatenate([maskf[0:1], maskf[1:2]], axis=1)

    lane, col = grid_of(128, 128)
    by_q = onehot((lane % 16 == col // 8) & (lane // 16 == col % 8))
    q_by = onehot((col % 16 == lane // 8) & (col // 16 == lane % 8))

    def edge(w):
        both = mm(w, zn, TT)
        return jax.nn.sigmoid(both[:128]) * both[128:] * mask_row

    left = edge(wl_ref[...]).astype(BF16)
    for ii in range(2):
        send_l[:, ii] = left[:, ii * 256 : (ii + 1) * 256].reshape(NY, 16, 256)
    pl.semaphore_wait(barrier, NY + NQ - 2)
    send_y(lambda to: send_l.at[to], got_l, 0)
    for load in loads[3:]:
        load.wait()
    wr = jnp.concatenate([mm(wr_ref[:, :128], by_q), mm(wr_ref[:, 128:], by_q)], axis=1).astype(BF16)
    right = edge(wr)
    right = jnp.stack([right[:, :256].reshape(NQ, 8, 256), right[:, 256:].reshape(NQ, 8, 256)], axis=1)
    send_r[...] = right.reshape(NQ, 16, 256).astype(BF16)
    send_q(lambda to: send_r.at[to], got_r, 1)
    got_l[y] = send_l[y]
    got_r[q] = send_r[q]

    r, s = grid_of(256, 256)
    turn = onehot((r // 16 == s % 16) & ((r // 8) % 2 == (s // 16) % 2) & (r % 8 == s // 32))
    back = onehot((s // 16 == r % 16) & ((s // 8) % 2 == (r // 16) % 2) & (s % 8 == r // 32))

    arrive(1)
    next_r[...] = mm(back, got_r[...].reshape(256, 256)).astype(BF16).reshape(NY, 32, 256)
    send_y(lambda to: next_r.at[to], have_r, 5)
    arrive(0)
    next_l[...] = mm(turn, got_l[...].reshape(256, 256)).astype(BF16).reshape(NQ, 16, 256)
    send_q(lambda to: next_l.at[to], have_l, 4)
    have_l[q] = next_l[q]
    have_r[y] = next_r[y]

    rows0 = jnp.where(lane % 2 == 0, maskf[0:1, :128], maskf[0:1, 128:])
    rows1 = jnp.where(lane % 2 == 0, maskf[1:2, :128], maskf[1:2, 128:])
    eye = onehot(lane == col)
    spread = jnp.where(lane < 64, rows0, rows1).astype(BF16)
    send_m[...] = mm(eye, spread, NT).astype(BF16).reshape(NY, 16, 128)
    send_y(lambda to: pair_in.at[:, :, to], got_p, 2)
    send_y(lambda to: send_m.at[to], got_m, 3)
    got_p[y] = pair_ref[:, :, y]
    got_m[y] = send_m[y]

    arrive(5)
    arrive(4)
    tri = mm(have_r[...].reshape(256, 256), have_l[...].reshape(256, 256), NT)
    send_t[...] = tri.astype(BF16).reshape(NY, 32, 256)
    send_y(lambda to: send_t.at[to], got_t, 7)
    got_t[y] = send_t[y]

    arrive(2)
    arrive(3)
    m0 = got_m[...].astype(F32)
    m1 = pltpu.roll(m0.reshape(128, 128), 64, 1).reshape(NY, 16, 128)
    m01 = jnp.stack([m0, m1], axis=1).reshape(256, 128).astype(BF16)
    m01 = mm(turn, m01).astype(BF16).reshape(8, 2, 16, 128)
    for z in range(2):
        part = mm(turn, got_p[:, :, z].reshape(256, 128)).astype(BF16)
        next_p[z * 8 : z * 8 + 8, 0:2] = part.reshape(8, 2, 16, 128)
        next_p[z * 8 : z * 8 + 8, 2:4] = m01
    send_q(lambda to: next_p.at[to], have_p, 6)
    have_p[q] = next_p[q]

    arrive(6)
    pairs, gates, lives = [], [], []
    pick = onehot(lane == zl)
    for jj in range(2):
        p = have_p[:, jj].reshape(256, 128).astype(F32)
        zc = norm(p, 1).astype(BF16)
        pairs.append(p)
        gates.append(jax.nn.sigmoid(mm(zc, wg_ref[...])))
        lives.append(mm(have_p[:, 2 + jj].reshape(256, 128), pick))
    wa = wa_ref[...]
    wk = wa[:, 128:256]
    wq_t, wv_t, wgate_t = wa[:, :128], wa[:, 256:384], wa[:, 384:]

    arrive(7)
    next_t[...] = mm(turn, got_t[...].reshape(256, 256)).astype(BF16).reshape(NQ, 16, 256)
    send_q(lambda to: next_t.at[to], have_t, 8)
    have_t[q] = next_t[q]
    wo = mm(q_by, wo_ref[...]).astype(BF16)
    order = onehot(
        (col // 16 == lane % 8)
        & ((col // 8) % 2 == lane // 64)
        & ((col // 4) % 2 == (lane // 8) % 2)
        & (col % 4 == (lane // 16) % 4)
    )
    arrive(8)

    pair1, yns = [], []
    tris = have_t[...].astype(F32).reshape(NQ, 2, 8, 256)
    for jj in range(2):
        t = tris[:, jj].reshape(128, 256)
        tn = norm(t, 0).astype(BF16)
        p1 = pairs[jj] + gates[jj] * mm(tn, wo, YN)
        pair1.append(p1)
        yns.append(norm(p1, 1).astype(BF16))

    parts = [mm(wb_ref[...], yn, NT) for yn in yns]
    both = jnp.concatenate(parts, axis=0)
    send_b[...] = jnp.concatenate([both[:, :128], both[:, 128:]], axis=0).astype(BF16)
    send_y(lambda to: send_b, got_b, 9)
    got_b[y] = send_b[...]

    keys, queries, values, out_gates = [], [], [], []
    for jj in range(2):
        keys.append(mm(yns[jj], wk).astype(BF16))
        queries.append(mm(wq_t, yns[jj], TT).astype(BF16))
        values.append(mm(wv_t, yns[jj], TT).astype(BF16))
        out_gates.append(jax.nn.sigmoid(mm(wgate_t, yns[jj], TT)))

    arrive(9)
    next_b[...] = mm(order, got_b[...].reshape(128, 128)).astype(BF16).reshape(8, 16, 128)
    near = moved(q, (0, 0, 1))
    for k, step in enumerate(FAR_CHIP):
        sent[10 + k] = have_b.at[0]
        to = moved(q, step)
        send(next_b, have_b.at[q], 10 + k, device_of(to, y))
    have_b[q] = next_b[...]
    sent[17] = due[17] = have_b.at[pl.ds(0, 8)]
    send(next_b, have_b.at[q], 17, device_of(near, y))

    head_row = lax.broadcasted_iota(jnp.int32, (128, 256), 0) // 32
    scale = F32(32.0**-0.5)
    for jj in range(2):
        for h in range(4):
            qh = jnp.where(head_row == h, queries[jj].astype(F32), F32(0)).astype(BF16)
            scores[jj, h] = mm(keys[jj], qh) * scale

    for k in reversed(range(7)):
        dz, dx, _ = FAR_CHIP[k]
        at = moved(q, (dz, -dx, 0))
        wait_on(have_b.at[0], rsem.at[10 + k])
        send(have_b.at[at], have_b.at[at], 17, device_of(near, y))
    arrive(17)
    atts = [[], []]
    for h in range(4):
        bias = jnp.concatenate(
            [mm(eye, have_b[:, kh * 4 + h].reshape(256, 128), NT) for kh in range(2)], axis=0
        )
        for jj in range(2):
            live = jnp.concatenate([lives[jj], lives[jj]], axis=1) > 0.5
            sc = jnp.where(live, scores[jj, h] + bias, F32(-1e9))
            e = jnp.exp(sc - jnp.max(sc, axis=0, keepdims=True))
            w = (e / jnp.sum(e, axis=0, keepdims=True)).astype(BF16)
            o = mm(values[jj][h * 32 : (h + 1) * 32], w)
            atts[jj].append(out_gates[jj][h * 32 : (h + 1) * 32] * o)
    for jj in range(2):
        att = jnp.concatenate(atts[jj], axis=0).astype(BF16)
        res = pair1[jj] + mm(att, wao_ref[...], YN)
        for qq in range(NQ):
            for ii in range(2):
                start = (qq // 8) * 256 + (qq % 8) * 4 + ii * 2 + jj
                out_ref[pl.ds(start, 8, stride=32), :] = res[qq * 16 + ii * 8 : qq * 16 + ii * 8 + 8]

    for k, ref in sent.items():
        wait_on(ref, ssem.at[k])


def shards(pair, pair_mask, wl, wr, wg, wo, wa, wb, wao):
    vm = pl.BlockSpec(memory_space=pltpu.VMEM)
    hbm = pl.BlockSpec(memory_space=pltpu.HBM)
    out = pl.pallas_call(
        kernel,
        out_shape=jax.ShapeDtypeStruct((512, 128), F32),
        in_specs=[hbm] * 9,
        out_specs=vm,
        scratch_shapes=[
            pltpu.VMEM((2, 2, 8, 16, 128), BF16),
            pltpu.VMEM((2, 256), jnp.int32),
            pltpu.VMEM((128, 256), BF16),
            pltpu.VMEM((128, 256), BF16),
            pltpu.VMEM((128, 128), BF16),
            pltpu.VMEM((128, 128), BF16),
            pltpu.VMEM((128, 512), BF16),
            pltpu.VMEM((4, 128), BF16),
            pltpu.VMEM((128, 128), BF16),
            pltpu.VMEM((NY, 2, 16, 256), BF16),
            pltpu.VMEM((NQ, 16, 256), BF16),
            pltpu.VMEM((NY, 16, 128), BF16),
            pltpu.VMEM((NY, 2, 16, 256), BF16),
            pltpu.VMEM((NQ, 16, 256), BF16),
            pltpu.VMEM((NY, 2, 2, 16, 128), BF16),
            pltpu.VMEM((NY, 16, 128), BF16),
            pltpu.VMEM((NQ, 16, 256), BF16),
            pltpu.VMEM((NY, 32, 256), BF16),
            pltpu.VMEM((NQ, 4, 16, 128), BF16),
            pltpu.VMEM((NQ, 16, 256), BF16),
            pltpu.VMEM((NY, 32, 256), BF16),
            pltpu.VMEM((NQ, 4, 16, 128), BF16),
            pltpu.VMEM((NY, 32, 256), BF16),
            pltpu.VMEM((NY, 32, 256), BF16),
            pltpu.VMEM((NQ, 16, 256), BF16),
            pltpu.VMEM((NQ, 16, 256), BF16),
            pltpu.VMEM((16, 128), BF16),
            pltpu.VMEM((NY, 16, 128), BF16),
            pltpu.VMEM((8, 16, 128), BF16),
            pltpu.VMEM((NQ, 8, 16, 128), BF16),
            pltpu.VMEM((2, 4, 256, 256), F32),
            pltpu.SemaphoreType.DMA((18,)),
            pltpu.SemaphoreType.DMA((18,)),
            pltpu.SemaphoreType.DMA((9,)),
        ],
        compiler_params=pltpu.CompilerParams(
            collective_id=0, has_side_effects=True, vmem_limit_bytes=60 * 1024 * 1024
        ),
    )(pair.reshape(2, 2, 8, 16, 128), pair_mask, wl, wr, wg, wo, wa, wb.T, wao)
    return out.reshape(256, 2, 128)


def solution(mesh):
    rows = ("dp", "dap")
    return jax.shard_map(
        shards,
        mesh=mesh,
        in_specs=(P(rows, None, None), P(rows, None), P(), P(), P(), P(), P(), P(), P()),
        out_specs=P("dp", "dap", None),
        check_vma=False,
    )
```

```python
import itertools

import jax
import jax.numpy as jnp
from jax import lax
from jax.experimental import pallas as pl
from jax.experimental.pallas import tpu as pltpu
from jax.sharding import PartitionSpec as P

MESH = pl.DeviceIdType.MESH
BF16 = jnp.bfloat16
F32 = jnp.float32
NY = 8
NQ = 16
YN = (((0,), (0,)), ((), ()))
NT = (((1,), (1,)), ((), ()))
TT = (((0,), (1,)), ((), ()))


FAR_Y = (4, 3, 5, 2, 6, 1, 7)
FAR_Q = tuple((dz, dx, dc) for dz, dx in ((1, 2), (1, 1), (1, 3), (0, 2), (0, 1), (0, 3), (1, 0)) for dc in (0, 1)) + ((0, 0, 1),)
FAR_ALL = tuple(
    sorted(
        (s for s in itertools.product(range(2), range(8), range(4), range(2)) if any(s)),
        key=lambda s: -(s[0] + min(s[1], 8 - s[1]) + min(s[2], 4 - s[2]) + 0.1 * s[3]),
    )
)


def device_of(q, y):
    return (q // 8) * 64 + y * 8 + q % 8


def moved(q, step):
    dz, dx, dc = step
    return ((q // 8 + dz) % 2) * 8 + ((q // 2 + dx) % 4) * 2 + (q + dc) % 2


def mm(a, b, dims=(((1,), (0,)), ((), ()))):
    return lax.dot_general(a, b, dims, preferred_element_type=F32)


def norm(x, axis):
    mean = jnp.mean(x, axis=axis, keepdims=True)
    d = x - mean
    var = jnp.mean(d * d, axis=axis, keepdims=True)
    return d * lax.rsqrt(var + 1e-05)


def grid_of(n, m):
    return (
        lax.broadcasted_iota(jnp.int32, (n, m), 0),
        lax.broadcasted_iota(jnp.int32, (n, m), 1),
    )


def onehot(cond):
    return jnp.where(cond, F32(1), F32(0)).astype(BF16)


def kernel(
    pair_in, mask_in, wl_in, wr_in, wg_in, wo_in, wa_in, wb_in, wao_in, out_ref,
    pair_ref, mask_ref, wl_ref, wr_ref, wg_ref, wo_ref, wa_ref, wb_ref, wao_ref,
    send_l, send_r, send_m, got_l, got_r, got_p, got_m,
    next_l, next_r, next_p, have_l, have_r, have_p,
    send_t, have_t, send_b, have_b, scores, ssem, rsem, lsem,
):
    me = lax.axis_index("dap")
    zl, y, xc = me // 64, (me // 8) % 8, me % 8
    q = zl * 8 + xc

    loads = [
        pltpu.make_async_copy(a, b, lsem.at[k])
        for k, (a, b) in enumerate((
            (pair_in, pair_ref), (wl_in, wl_ref), (mask_in, mask_ref), (wr_in, wr_ref), (wg_in, wg_ref),
            (wo_in, wo_ref), (wa_in, wa_ref), (wb_in, wb_ref), (wao_in, wao_ref),
        ))
    ]
    for load in loads:
        load.start()
    barrier = pltpu.get_barrier_semaphore()

    peers = [device_of(q, (y + s) % NY) for s in FAR_Y] + [device_of(moved(q, step), y) for step in FAR_Q]
    for peer in peers:
        pl.semaphore_signal(barrier, inc=1, device_id={"dap": peer}, device_id_type=MESH)

    sent, due = {}, {}
    near = moved(q, (0, 0, 1))

    def send(src, dst, k, peer):
        pltpu.make_async_remote_copy(
            src_ref=src, dst_ref=dst, send_sem=ssem.at[k], recv_sem=rsem.at[k],
            device_id={"dap": peer}, device_id_type=MESH,
        ).start()

    def send_y(src, dst, k):
        sent[k] = due[k] = dst.at[pl.ds(0, NY - 1)]
        for s in FAR_Y:
            to = (y + s) % NY
            send(src(to), dst.at[y], k, device_of(q, to))

    def send_q(src, dst, k):
        sent[k] = due[k] = dst.at[pl.ds(0, NQ - 1)]
        for step in FAR_Q:
            to = moved(q, step)
            send(src(to), dst.at[q], k, device_of(to, y))

    def wait_on(ref, sem):
        pltpu.make_async_copy(ref, ref, sem).wait()

    def arrive(k):
        wait_on(due.pop(k), rsem.at[k])

    for load in loads[:3]:
        load.wait()
    x = pair_ref[...].astype(F32).reshape(512, 128)
    zn = norm(x, 1).astype(BF16)
    maskf = mask_ref[...].astype(F32)
    mask_row = jnp.concatenate([maskf[0:1], maskf[1:2]], axis=1)

    lane, col = grid_of(128, 128)
    by_q = onehot((lane % 16 == col // 8) & (lane // 16 == col % 8))

    def edge(w):
        both = mm(w, zn, TT)
        return jax.nn.sigmoid(both[:128]) * both[128:] * mask_row

    left = edge(wl_ref[...]).astype(BF16)
    for ii in range(2):
        send_l[:, ii] = left[:, ii * 256 : (ii + 1) * 256].reshape(NY, 16, 256)
    pl.semaphore_wait(barrier, NY + NQ - 2)
    send_y(lambda to: send_l.at[to], got_l, 0)
    for load in loads[3:]:
        load.wait()
    wr = jnp.concatenate([mm(wr_ref[:, :128], by_q), mm(wr_ref[:, 128:], by_q)], axis=1).astype(BF16)
    right = edge(wr)
    right = jnp.stack([right[:, :256].reshape(NQ, 8, 256), right[:, 256:].reshape(NQ, 8, 256)], axis=1)
    send_r[...] = right.reshape(NQ, 16, 256).astype(BF16)
    send_q(lambda to: send_r.at[to], got_r, 1)
    got_l[y] = send_l[y]
    got_r[q] = send_r[q]

    r, s = grid_of(256, 256)
    turn = onehot((r // 16 == s % 16) & ((r // 8) % 2 == (s // 16) % 2) & (r % 8 == s // 32))
    split = onehot((r % 2 == (s // 8) % 2) & ((r // 2) % 16 == s // 16) & (r // 32 == s % 8))
    twice = onehot(lax.broadcasted_iota(jnp.int32, (512, 256), 0) // 2 == lax.broadcasted_iota(jnp.int32, (512, 256), 1))
    even = lax.broadcasted_iota(jnp.int32, (512, 128), 0) % 2 == 0
    gather = onehot((s % 4 == r // 64) & (s // 4 == r % 64))

    arrive(1)
    next_r[...] = mm(split, got_r[...].reshape(256, 256)).astype(BF16).reshape(NY, 32, 256)
    send_y(lambda to: next_r.at[to], have_r, 5)
    arrive(0)
    next_l[...] = mm(turn, got_l[...].reshape(256, 256)).astype(BF16).reshape(NQ, 16, 256)
    send_q(lambda to: next_l.at[to], have_l, 4)
    have_l[q] = next_l[q]
    have_r[y] = next_r[y]

    rows0 = jnp.where(lane % 2 == 0, maskf[0:1, :128], maskf[0:1, 128:])
    rows1 = jnp.where(lane % 2 == 0, maskf[1:2, :128], maskf[1:2, 128:])
    eye = onehot(lane == col)
    spread = jnp.where(lane < 64, rows0, rows1).astype(BF16)
    send_m[...] = mm(eye, spread, NT).astype(BF16).reshape(NY, 16, 128)
    send_y(lambda to: pair_in.at[:, :, to], got_p, 2)
    send_y(lambda to: send_m.at[to], got_m, 3)
    got_p[y] = pair_ref[:, :, y]
    got_m[y] = send_m[y]

    arrive(5)
    doubled = mm(twice, have_r[...].reshape(256, 256)).astype(BF16)
    arrive(4)
    tri = mm(doubled, have_l[...].reshape(256, 256), NT)
    tri = jnp.where(even, tri[:, :128], tri[:, 128:])
    send_t[...] = tri.reshape(128, 4, 128).astype(BF16)
    sent[7] = due[7] = have_t.at[pl.ds(0, 127)]
    place = y * 16 + q
    for step in FAR_ALL:
        to, there = moved(q, (step[0], step[2], step[3])), (y + step[1]) % NY
        send(send_t.at[there * 16 + to], have_t.at[place], 7, device_of(to, there))
    have_t[place] = send_t[place]

    arrive(2)
    arrive(3)
    m0 = got_m[...].astype(F32)
    m1 = pltpu.roll(m0.reshape(128, 128), 64, 1).reshape(NY, 16, 128)
    m01 = jnp.stack([m0, m1], axis=1).reshape(256, 128).astype(BF16)
    m01 = mm(turn, m01).astype(BF16).reshape(8, 2, 16, 128)
    for z in range(2):
        part = mm(turn, got_p[:, :, z].reshape(256, 128)).astype(BF16)
        next_p[z * 8 : z * 8 + 8, 0:2] = part.reshape(8, 2, 16, 128)
        next_p[z * 8 : z * 8 + 8, 2:4] = m01
    send_q(lambda to: next_p.at[to], have_p, 6)
    have_p[q] = next_p[q]

    arrive(6)
    pairs, gates, lives = [], [], []
    pick = onehot(lane == zl)
    for jj in range(2):
        p = have_p[:, jj].reshape(256, 128).astype(F32)
        zc = norm(p, 1).astype(BF16)
        pairs.append(p)
        gates.append(jax.nn.sigmoid(mm(zc, wg_ref[...])))
        lives.append(mm(have_p[:, 2 + jj].reshape(256, 128), pick))
    wa = wa_ref[...]
    wk = wa[:, 128:256]
    wq_t, wv_t, wgate_t = wa[:, :128], wa[:, 256:384], wa[:, 384:]

    order = onehot(
        (s // 128 == (r // 16) % 2)
        & ((s // 16) % 8 == r % 8)
        & ((s // 8) % 2 == r // 128)
        & ((s // 4) % 2 == (r // 8) % 2)
        & (s % 4 == (r // 32) % 4)
    )
    arrive(7)

    pair1, yns = [], []
    tris = [mm(gather, have_t[b * 64 : b * 64 + 64].reshape(256, 128)).reshape(4, 64, 128) for b in range(2)]
    for jj in range(2):
        t = jnp.concatenate(
            [jnp.concatenate([tris[b][jj * 2 + half] for b in range(2)], axis=0) for half in range(2)], axis=1
        )
        tn = norm(t, 0).astype(BF16)
        p1 = pairs[jj] + gates[jj] * mm(tn, wo_ref[...], YN)
        pair1.append(p1)
        yns.append(norm(p1, 1).astype(BF16))

    parts = [mm(wb_ref[...], yn, NT) for yn in yns]
    both = jnp.concatenate(parts, axis=0)
    send_b[...] = jnp.concatenate([both[:, :128], both[:, 128:]], axis=0).astype(BF16)
    chip, core = q // 2, q % 2
    for step in FAR_ALL:
        if step[3] == 0:
            to, there = moved(q, (step[0], step[2], 0)), (y + step[1]) % NY
            send(send_b, have_b.at[chip, core, y], 9 + step[1], device_of(to, there))
    have_b[chip, core, y] = send_b[...]
    for k in range(NY):
        sent[9 + k] = have_b.at[pl.ds(0, 8 if k else 7), 0, 0]

    keys, queries, values, out_gates = [], [], [], []
    for jj in range(2):
        keys.append(mm(yns[jj], wk).astype(BF16))
        queries.append(mm(wq_t, yns[jj], TT).astype(BF16))
        values.append(mm(wv_t, yns[jj], TT).astype(BF16))
        out_gates.append(jax.nn.sigmoid(mm(wgate_t, yns[jj], TT)))

    head_row = lax.broadcasted_iota(jnp.int32, (128, 256), 0) // 32
    scale = F32(32.0**-0.5)
    for jj in range(2):
        for h in range(4):
            qh = jnp.where(head_row == h, queries[jj].astype(F32), F32(0)).astype(BF16)
            scores[jj, h] = mm(keys[jj], qh) * scale

    sent[17] = due[17] = have_b.at[:, 0]
    for k in (0, 1, 7, 2, 6, 3, 5, 4):
        wait_on(sent[9 + k], rsem.at[9 + k])
        block = have_b.at[:, core, (y + NY - k) % NY]
        send(block, block, 17, device_of(near, y))
    arrive(17)
    biases = [mm(order, have_b[b].reshape(256, 128)).astype(BF16).reshape(8, 32, 128) for b in range(8)]
    atts = [[], []]
    for h in range(4):
        bias = jnp.concatenate(
            [mm(eye, jnp.concatenate([b[kh * 4 + h] for b in biases], axis=0), NT) for kh in range(2)], axis=0
        )
        for jj in range(2):
            live = jnp.concatenate([lives[jj], lives[jj]], axis=1) > 0.5
            sc = jnp.where(live, scores[jj, h] + bias, F32(-1e9))
            e = jnp.exp(sc - jnp.max(sc, axis=0, keepdims=True))
            w = (e / jnp.sum(e, axis=0, keepdims=True)).astype(BF16)
            o = mm(values[jj][h * 32 : (h + 1) * 32], w)
            atts[jj].append(out_gates[jj][h * 32 : (h + 1) * 32] * o)
    for jj in range(2):
        att = jnp.concatenate(atts[jj], axis=0).astype(BF16)
        res = pair1[jj] + mm(att, wao_ref[...], YN)
        for qq in range(NQ):
            for ii in range(2):
                start = (qq // 8) * 256 + (qq % 8) * 4 + ii * 2 + jj
                out_ref[pl.ds(start, 8, stride=32), :] = res[qq * 16 + ii * 8 : qq * 16 + ii * 8 + 8]

    for k, ref in sent.items():
        wait_on(ref, ssem.at[k])


def shards(pair, pair_mask, wl, wr, wg, wo, wa, wb, wao):
    vm = pl.BlockSpec(memory_space=pltpu.VMEM)
    hbm = pl.BlockSpec(memory_space=pltpu.HBM)
    out = pl.pallas_call(
        kernel,
        out_shape=jax.ShapeDtypeStruct((512, 128), F32),
        in_specs=[hbm] * 9,
        out_specs=vm,
        scratch_shapes=[
            pltpu.VMEM((2, 2, 8, 16, 128), BF16),
            pltpu.VMEM((2, 256), jnp.int32),
            pltpu.VMEM((128, 256), BF16),
            pltpu.VMEM((128, 256), BF16),
            pltpu.VMEM((128, 128), BF16),
            pltpu.VMEM((128, 128), BF16),
            pltpu.VMEM((128, 512), BF16),
            pltpu.VMEM((4, 128), BF16),
            pltpu.VMEM((128, 128), BF16),
            pltpu.VMEM((NY, 2, 16, 256), BF16),
            pltpu.VMEM((NQ, 16, 256), BF16),
            pltpu.VMEM((NY, 16, 128), BF16),
            pltpu.VMEM((NY, 2, 16, 256), BF16),
            pltpu.VMEM((NQ, 16, 256), BF16),
            pltpu.VMEM((NY, 2, 2, 16, 128), BF16),
            pltpu.VMEM((NY, 16, 128), BF16),
            pltpu.VMEM((NQ, 16, 256), BF16),
            pltpu.VMEM((NY, 32, 256), BF16),
            pltpu.VMEM((NQ, 4, 16, 128), BF16),
            pltpu.VMEM((NQ, 16, 256), BF16),
            pltpu.VMEM((NY, 32, 256), BF16),
            pltpu.VMEM((NQ, 4, 16, 128), BF16),
            pltpu.VMEM((128, 4, 128), BF16),
            pltpu.VMEM((128, 4, 128), BF16),
            pltpu.VMEM((16, 128), BF16),
            pltpu.VMEM((8, 2, NY, 16, 128), BF16),
            pltpu.VMEM((2, 4, 256, 256), F32),
            pltpu.SemaphoreType.DMA((18,)),
            pltpu.SemaphoreType.DMA((18,)),
            pltpu.SemaphoreType.DMA((9,)),
        ],
        compiler_params=pltpu.CompilerParams(
            collective_id=0, has_side_effects=True, vmem_limit_bytes=60 * 1024 * 1024
        ),
    )(pair.reshape(2, 2, 8, 16, 128), pair_mask, wl, wr, wg, wo, wa, wb.T, wao)
    return out.reshape(256, 2, 128)


def solution(mesh):
    rows = ("dp", "dap")
    return jax.shard_map(
        shards,
        mesh=mesh,
        in_specs=(P(rows, None, None), P(rows, None), P(), P(), P(), P(), P(), P(), P()),
        out_specs=P("dp", "dap", None),
        check_vma=False,
    )
```

```python
import itertools

import jax
import jax.numpy as jnp
from jax import lax
from jax.experimental import pallas as pl
from jax.experimental.pallas import tpu as pltpu
from jax.sharding import PartitionSpec as P

MESH = pl.DeviceIdType.MESH
BF16 = jnp.bfloat16
F32 = jnp.float32
NY = 8
NQ = 16
YN = (((0,), (0,)), ((), ()))
NT = (((1,), (1,)), ((), ()))
TT = (((0,), (1,)), ((), ()))


FAR_Y = (4, 3, 5, 2, 6, 1, 7)
FAR_Q = tuple((dz, dx, dc) for dz, dx in ((1, 2), (1, 1), (1, 3), (0, 2), (0, 1), (0, 3), (1, 0)) for dc in (0, 1)) + ((0, 0, 1),)
FAR_ALL = tuple(
    sorted(
        (s for s in itertools.product(range(2), range(8), range(4), range(2)) if any(s)),
        key=lambda s: -(s[0] + min(s[1], 8 - s[1]) + min(s[2], 4 - s[2]) + 0.1 * s[3]),
    )
)


def device_of(q, y):
    return (q // 8) * 64 + y * 8 + q % 8


def moved(q, step):
    dz, dx, dc = step
    return ((q // 8 + dz) % 2) * 8 + ((q // 2 + dx) % 4) * 2 + (q + dc) % 2


def mm(a, b, dims=(((1,), (0,)), ((), ()))):
    return lax.dot_general(a, b, dims, preferred_element_type=F32)


def norm(x, axis):
    mean = jnp.mean(x, axis=axis, keepdims=True)
    d = x - mean
    var = jnp.mean(d * d, axis=axis, keepdims=True)
    return d * lax.rsqrt(var + 1e-05)


def grid_of(n, m):
    return (
        lax.broadcasted_iota(jnp.int32, (n, m), 0),
        lax.broadcasted_iota(jnp.int32, (n, m), 1),
    )


def onehot(cond):
    return jnp.where(cond, F32(1), F32(0)).astype(BF16)


def kernel(
    pair_in, mask_in, wl_in, wr_in, wg_in, wo_in, wa_in, wb_in, wao_in, out_ref,
    pair_ref, mask_ref, wl_ref, wr_ref, wg_ref, wo_ref, wa_ref, wb_ref, wao_ref,
    send_l, send_r, send_m, got_l, got_r, got_p, got_m,
    next_l, next_r, next_p, have_l, have_r, have_p,
    send_t, have_t, send_b, have_b, scores, ssem, rsem, lsem,
):
    me = lax.axis_index("dap")
    zl, y, xc = me // 64, (me // 8) % 8, me % 8
    q = zl * 8 + xc

    loads = [
        pltpu.make_async_copy(a, b, lsem.at[k])
        for k, (a, b) in enumerate((
            (pair_in, pair_ref), (wl_in, wl_ref), (mask_in, mask_ref), (wr_in, wr_ref), (wg_in, wg_ref),
            (wo_in, wo_ref), (wa_in, wa_ref), (wb_in, wb_ref), (wao_in, wao_ref),
        ))
    ]
    for load in loads:
        load.start()
    barrier = pltpu.get_barrier_semaphore()

    peers = [device_of(q, (y + s) % NY) for s in FAR_Y] + [device_of(moved(q, step), y) for step in FAR_Q]
    for peer in peers:
        pl.semaphore_signal(barrier, inc=1, device_id={"dap": peer}, device_id_type=MESH)

    sent, due = {}, {}
    near = moved(q, (0, 0, 1))

    def send(src, dst, k, peer):
        pltpu.make_async_remote_copy(
            src_ref=src, dst_ref=dst, send_sem=ssem.at[k], recv_sem=rsem.at[k],
            device_id={"dap": peer}, device_id_type=MESH,
        ).start()

    def send_y(src, dst, k):
        sent[k] = due[k] = dst.at[pl.ds(0, NY - 1)]
        for s in FAR_Y:
            to = (y + s) % NY
            send(src(to), dst.at[y], k, device_of(q, to))

    def send_q(src, dst, k):
        sent[k] = due[k] = dst.at[pl.ds(0, NQ - 1)]
        for step in FAR_Q:
            to = moved(q, step)
            send(src(to), dst.at[q], k, device_of(to, y))

    def wait_on(ref, sem):
        pltpu.make_async_copy(ref, ref, sem).wait()

    def arrive(k):
        wait_on(due.pop(k), rsem.at[k])

    for load in loads[:3]:
        load.wait()
    x = pair_ref[...].astype(F32).reshape(512, 128)
    zn = norm(x, 1).astype(BF16)
    maskf = mask_ref[...].astype(F32)
    mask_row = jnp.concatenate([maskf[0:1], maskf[1:2]], axis=1)

    lane, col = grid_of(128, 128)
    by_q = onehot((lane % 16 == col // 8) & (lane // 16 == col % 8))

    def edge(w):
        both = mm(w, zn, TT)
        return jax.nn.sigmoid(both[:128]) * both[128:] * mask_row

    left = edge(wl_ref[...]).astype(BF16)
    for ii in range(2):
        send_l[:, ii] = left[:, ii * 256 : (ii + 1) * 256].reshape(NY, 16, 256)
    pl.semaphore_wait(barrier, NY + NQ - 2)
    send_y(lambda to: send_l.at[to], got_l, 0)
    for load in loads[3:]:
        load.wait()
    wr = jnp.concatenate([mm(wr_ref[:, :128], by_q), mm(wr_ref[:, 128:], by_q)], axis=1).astype(BF16)
    right = edge(wr)
    right = jnp.stack([right[:, :256].reshape(NQ, 8, 256), right[:, 256:].reshape(NQ, 8, 256)], axis=1)
    send_r[...] = right.reshape(NQ, 16, 256).astype(BF16)
    send_q(lambda to: send_r.at[to], got_r, 1)
    got_l[y] = send_l[y]
    got_r[q] = send_r[q]

    rows0 = jnp.where(lane % 2 == 0, maskf[0:1, :128], maskf[0:1, 128:])
    rows1 = jnp.where(lane % 2 == 0, maskf[1:2, :128], maskf[1:2, 128:])
    eye = onehot(lane == col)
    spread = jnp.where(lane < 64, rows0, rows1).astype(BF16)
    send_m[...] = mm(eye, spread, NT).astype(BF16).reshape(NY, 16, 128)
    send_y(lambda to: pair_in.at[:, :, to], got_p, 2)
    send_y(lambda to: send_m.at[to], got_m, 3)
    got_p[y] = pair_ref[:, :, y]
    got_m[y] = send_m[y]

    r, s = grid_of(256, 256)
    turn = onehot((r // 16 == s % 16) & ((r // 8) % 2 == (s // 16) % 2) & (r % 8 == s // 32))
    split = onehot((r % 2 == (s // 8) % 2) & ((r // 2) % 16 == s // 16) & (r // 32 == s % 8))
    twice = onehot(lax.broadcasted_iota(jnp.int32, (512, 256), 0) // 2 == lax.broadcasted_iota(jnp.int32, (512, 256), 1))
    even = lax.broadcasted_iota(jnp.int32, (512, 128), 0) % 2 == 0
    gather = onehot((s % 4 == r // 64) & (s // 4 == r % 64))

    arrive(1)
    next_r[...] = mm(split, got_r[...].reshape(256, 256)).astype(BF16).reshape(NY, 32, 256)
    send_y(lambda to: next_r.at[to], have_r, 5)
    arrive(0)
    next_l[...] = mm(turn, got_l[...].reshape(256, 256)).astype(BF16).reshape(NQ, 16, 256)
    send_q(lambda to: next_l.at[to], have_l, 4)
    have_l[q] = next_l[q]
    have_r[y] = next_r[y]

    arrive(5)
    doubled = mm(twice, have_r[...].reshape(256, 256)).astype(BF16)
    arrive(4)
    tri = mm(doubled, have_l[...].reshape(256, 256), NT)
    tri = jnp.where(even, tri[:, :128], tri[:, 128:])
    send_t[...] = tri.reshape(128, 4, 128).astype(BF16)
    sent[7] = due[7] = have_t.at[pl.ds(0, 127)]
    place = y * 16 + q
    for step in FAR_ALL:
        to, there = moved(q, (step[0], step[2], step[3])), (y + step[1]) % NY
        send(send_t.at[there * 16 + to], have_t.at[place], 7, device_of(to, there))
    have_t[place] = send_t[place]

    arrive(2)
    arrive(3)
    m0 = got_m[...].astype(F32)
    m1 = pltpu.roll(m0.reshape(128, 128), 64, 1).reshape(NY, 16, 128)
    m01 = jnp.stack([m0, m1], axis=1).reshape(256, 128).astype(BF16)
    m01 = mm(turn, m01).astype(BF16).reshape(8, 2, 16, 128)
    for z in range(2):
        part = mm(turn, got_p[:, :, z].reshape(256, 128)).astype(BF16)
        next_p[z * 8 : z * 8 + 8, 0:2] = part.reshape(8, 2, 16, 128)
        next_p[z * 8 : z * 8 + 8, 2:4] = m01
    send_q(lambda to: next_p.at[to], have_p, 6)
    have_p[q] = next_p[q]

    arrive(6)
    pairs, gates, lives = [], [], []
    pick = onehot(lane == zl)
    for jj in range(2):
        p = have_p[:, jj].reshape(256, 128).astype(F32)
        zc = norm(p, 1).astype(BF16)
        pairs.append(p)
        gates.append(jax.nn.sigmoid(mm(zc, wg_ref[...])))
        lives.append(mm(have_p[:, 2 + jj].reshape(256, 128), pick))
    wa = wa_ref[...]
    wk = wa[:, 128:256]
    wq_t, wv_t, wgate_t = wa[:, :128], wa[:, 256:384], wa[:, 384:]

    order = onehot(
        (s // 128 == (r // 16) % 2)
        & ((s // 16) % 8 == r % 8)
        & ((s // 8) % 2 == r // 128)
        & ((s // 4) % 2 == (r // 8) % 2)
        & (s % 4 == (r // 32) % 4)
    )
    arrive(7)

    pair1, yns = [], []
    tris = [mm(gather, have_t[b * 64 : b * 64 + 64].reshape(256, 128)).reshape(4, 64, 128) for b in range(2)]
    for jj in range(2):
        t = jnp.concatenate(
            [jnp.concatenate([tris[b][jj * 2 + half] for b in range(2)], axis=0) for half in range(2)], axis=1
        )
        tn = norm(t, 0).astype(BF16)
        p1 = pairs[jj] + gates[jj] * mm(tn, wo_ref[...], YN)
        pair1.append(p1)
        yns.append(norm(p1, 1).astype(BF16))

    parts = [mm(wb_ref[...], yn, NT) for yn in yns]
    both = jnp.concatenate(parts, axis=0)
    send_b[...] = jnp.concatenate([both[:, :128], both[:, 128:]], axis=0).astype(BF16)
    chip, core = q // 2, q % 2
    for step in FAR_ALL:
        if step[3] == 0:
            to, there = moved(q, (step[0], step[2], 0)), (y + step[1]) % NY
            send(send_b, have_b.at[chip, core, y], 9 + step[1], device_of(to, there))
    have_b[chip, core, y] = send_b[...]
    for k in range(NY):
        sent[9 + k] = have_b.at[pl.ds(0, 8 if k else 7), 0, 0]

    keys, queries, values, out_gates = [], [], [], []
    for jj in range(2):
        keys.append(mm(yns[jj], wk).astype(BF16))
        queries.append(mm(wq_t, yns[jj], TT).astype(BF16))
        values.append(mm(wv_t, yns[jj], TT).astype(BF16))
        out_gates.append(jax.nn.sigmoid(mm(wgate_t, yns[jj], TT)))

    head_row = lax.broadcasted_iota(jnp.int32, (128, 256), 0) // 32
    scale = F32(32.0**-0.5)
    for jj in range(2):
        for h in range(4):
            qh = jnp.where(head_row == h, queries[jj].astype(F32), F32(0)).astype(BF16)
            scores[jj, h] = mm(keys[jj], qh) * scale

    sent[17] = due[17] = have_b.at[:, 0]
    for k in (0, 1, 7, 2, 6, 3, 5, 4):
        wait_on(sent[9 + k], rsem.at[9 + k])
        block = have_b.at[:, core, (y + NY - k) % NY]
        send(block, block, 17, device_of(near, y))
    arrive(17)
    biases = [mm(order, have_b[b].reshape(256, 128)).astype(BF16).reshape(8, 32, 128) for b in range(8)]
    atts = [[], []]
    for h in range(4):
        bias = jnp.concatenate(
            [mm(eye, jnp.concatenate([b[kh * 4 + h] for b in biases], axis=0), NT) for kh in range(2)], axis=0
        )
        for jj in range(2):
            live = jnp.concatenate([lives[jj], lives[jj]], axis=1) > 0.5
            sc = jnp.where(live, scores[jj, h] + bias, F32(-1e9))
            e = jnp.exp(sc - jnp.max(sc, axis=0, keepdims=True))
            w = (e / jnp.sum(e, axis=0, keepdims=True)).astype(BF16)
            o = mm(values[jj][h * 32 : (h + 1) * 32], w)
            atts[jj].append(out_gates[jj][h * 32 : (h + 1) * 32] * o)
    for jj in range(2):
        att = jnp.concatenate(atts[jj], axis=0).astype(BF16)
        res = pair1[jj] + mm(att, wao_ref[...], YN)
        for qq in range(NQ):
            for ii in range(2):
                start = (qq // 8) * 256 + (qq % 8) * 4 + ii * 2 + jj
                out_ref[pl.ds(start, 8, stride=32), :] = res[qq * 16 + ii * 8 : qq * 16 + ii * 8 + 8]

    for k, ref in sent.items():
        wait_on(ref, ssem.at[k])


def shards(pair, pair_mask, wl, wr, wg, wo, wa, wb, wao):
    vm = pl.BlockSpec(memory_space=pltpu.VMEM)
    hbm = pl.BlockSpec(memory_space=pltpu.HBM)
    inputs = (pair.reshape(2, 2, 8, 16, 128), pair_mask, wl, wr, wg, wo, wa, wb.T, wao)
    out = pl.pallas_call(
        kernel,
        out_shape=jax.ShapeDtypeStruct((512, 128), F32),
        in_specs=[hbm] * 9,
        out_specs=vm,
        scratch_shapes=[
            pltpu.VMEM((2, 2, 8, 16, 128), BF16),
            pltpu.VMEM((2, 256), jnp.int32),
            pltpu.VMEM((128, 256), BF16),
            pltpu.VMEM((128, 256), BF16),
            pltpu.VMEM((128, 128), BF16),
            pltpu.VMEM((128, 128), BF16),
            pltpu.VMEM((128, 512), BF16),
            pltpu.VMEM((4, 128), BF16),
            pltpu.VMEM((128, 128), BF16),
            pltpu.VMEM((NY, 2, 16, 256), BF16),
            pltpu.VMEM((NQ, 16, 256), BF16),
            pltpu.VMEM((NY, 16, 128), BF16),
            pltpu.VMEM((NY, 2, 16, 256), BF16),
            pltpu.VMEM((NQ, 16, 256), BF16),
            pltpu.VMEM((NY, 2, 2, 16, 128), BF16),
            pltpu.VMEM((NY, 16, 128), BF16),
            pltpu.VMEM((NQ, 16, 256), BF16),
            pltpu.VMEM((NY, 32, 256), BF16),
            pltpu.VMEM((NQ, 4, 16, 128), BF16),
            pltpu.VMEM((NQ, 16, 256), BF16),
            pltpu.VMEM((NY, 32, 256), BF16),
            pltpu.VMEM((NQ, 4, 16, 128), BF16),
            pltpu.VMEM((128, 4, 128), BF16),
            pltpu.VMEM((128, 4, 128), BF16),
            pltpu.VMEM((16, 128), BF16),
            pltpu.VMEM((8, 2, NY, 16, 128), BF16),
            pltpu.VMEM((2, 4, 256, 256), F32),
            pltpu.SemaphoreType.DMA((18,)),
            pltpu.SemaphoreType.DMA((18,)),
            pltpu.SemaphoreType.DMA((9,)),
        ],
        compiler_params=pltpu.CompilerParams(
            collective_id=0, has_side_effects=True, vmem_limit_bytes=32 * 1024 * 1024
        ),
    )(*(pltpu.with_memory_space_constraint(a, pltpu.HBM) for a in inputs))
    return out.reshape(256, 2, 128)


def solution(mesh):
    rows = ("dp", "dap")
    return jax.shard_map(
        shards,
        mesh=mesh,
        in_specs=(P(rows, None, None), P(rows, None), P(), P(), P(), P(), P(), P(), P()),
        out_specs=P("dp", "dap", None),
        check_vma=False,
    )
```

```python
import itertools

import jax
import jax.numpy as jnp
from jax import lax
from jax.experimental import pallas as pl
from jax.experimental.pallas import tpu as pltpu
from jax.sharding import PartitionSpec as P

MESH = pl.DeviceIdType.MESH
BF16 = jnp.bfloat16
F32 = jnp.float32
NY = 8
NQ = 16
YN = (((0,), (0,)), ((), ()))
NT = (((1,), (1,)), ((), ()))
TT = (((0,), (1,)), ((), ()))


FAR_Y = (4, 3, 5, 2, 6, 1, 7)
FAR_Q = tuple((dz, dx, dc) for dz, dx in ((1, 2), (1, 1), (1, 3), (0, 2), (0, 1), (0, 3), (1, 0)) for dc in (0, 1)) + ((0, 0, 1),)
FAR_ALL = tuple(
    sorted(
        (s for s in itertools.product(range(2), range(8), range(4), range(2)) if any(s)),
        key=lambda s: -(s[0] + min(s[1], 8 - s[1]) + min(s[2], 4 - s[2]) + 0.1 * s[3]),
    )
)


def device_of(q, y):
    return (q // 8) * 64 + y * 8 + q % 8


def moved(q, step):
    dz, dx, dc = step
    return ((q // 8 + dz) % 2) * 8 + ((q // 2 + dx) % 4) * 2 + (q + dc) % 2


def mm(a, b, dims=(((1,), (0,)), ((), ()))):
    return lax.dot_general(a, b, dims, preferred_element_type=F32)


def norm(x, axis):
    mean = jnp.mean(x, axis=axis, keepdims=True)
    d = x - mean
    var = jnp.mean(d * d, axis=axis, keepdims=True)
    return d * lax.rsqrt(var + 1e-05)


def grid_of(n, m):
    return (
        lax.broadcasted_iota(jnp.int32, (n, m), 0),
        lax.broadcasted_iota(jnp.int32, (n, m), 1),
    )


def onehot(cond):
    return jnp.where(cond, F32(1), F32(0)).astype(BF16)


def kernel(
    pair_in, mask_in, wl_in, wr_in, wg_in, wo_in, wa_in, wb_in, wao_in, out_ref,
    pair_ref, mask_ref, wl_ref, wr_ref, wg_ref, wo_ref, wa_ref, wb_ref, wao_ref,
    send_l, send_r, send_m, got_l, got_r, got_p, got_m,
    next_l, next_r, next_p, have_l, have_r, have_p,
    send_t, have_t, send_b, have_b, scores, ssem, rsem, lsem,
):
    me = lax.axis_index("dap")
    zl, y, xc = me // 64, (me // 8) % 8, me % 8
    q = zl * 8 + xc
    at_y = [(y + s) % NY for s in range(NY)]
    at_q = {}
    for dz, dx, dc in itertools.product(range(2), range(4), range(2)):
        z, xx, cc = (zl + dz) % 2, (q // 2 + dx) % 4 * 2, (q + dc) % 2
        at_q[dz, dx, dc] = (z * 8 + xx + cc, z * 64 + xx + cc)
    y_part = [v * 8 for v in at_y]
    y_slot = [v * 16 for v in at_y]

    loads = [
        pltpu.make_async_copy(a, b, lsem.at[k])
        for k, (a, b) in enumerate((
            (pair_in, pair_ref), (wl_in, wl_ref), (mask_in, mask_ref), (wr_in, wr_ref), (wg_in, wg_ref),
            (wo_in, wo_ref), (wa_in, wa_ref), (wb_in, wb_ref), (wao_in, wao_ref),
        ))
    ]
    for load in loads:
        load.start()
    barrier = pltpu.get_barrier_semaphore()

    peers = [device_of(q, (y + s) % NY) for s in FAR_Y] + [device_of(moved(q, step), y) for step in FAR_Q]
    for peer in peers:
        pl.semaphore_signal(barrier, inc=1, device_id={"dap": peer}, device_id_type=MESH)

    sent, due = {}, {}
    near = moved(q, (0, 0, 1))

    def send(src, dst, k, peer):
        pltpu.make_async_remote_copy(
            src_ref=src, dst_ref=dst, send_sem=ssem.at[k], recv_sem=rsem.at[k],
            device_id={"dap": peer}, device_id_type=MESH,
        ).start()

    def send_y(src, dst, k):
        sent[k] = due[k] = dst.at[pl.ds(0, NY - 1)]
        for s in FAR_Y:
            to = (y + s) % NY
            send(src(to), dst.at[y], k, device_of(q, to))

    def send_q(src, dst, k):
        sent[k] = due[k] = dst.at[pl.ds(0, NQ - 1)]
        for step in FAR_Q:
            to = moved(q, step)
            send(src(to), dst.at[q], k, device_of(to, y))

    def wait_on(ref, sem):
        pltpu.make_async_copy(ref, ref, sem).wait()

    def arrive(k):
        wait_on(due.pop(k), rsem.at[k])

    for load in loads[:3]:
        load.wait()
    x = pair_ref[...].astype(F32).reshape(512, 128)
    zn = norm(x, 1).astype(BF16)
    maskf = mask_ref[...].astype(F32)
    mask_row = jnp.concatenate([maskf[0:1], maskf[1:2]], axis=1)

    lane, col = grid_of(128, 128)
    by_q = onehot((lane % 16 == col // 8) & (lane // 16 == col % 8))

    def edge(w):
        both = mm(w, zn, TT)
        return jax.nn.sigmoid(both[:128]) * both[128:] * mask_row

    left = edge(wl_ref[...]).astype(BF16)
    for ii in range(2):
        send_l[:, ii] = left[:, ii * 256 : (ii + 1) * 256].reshape(NY, 16, 256)
    pl.semaphore_wait(barrier, NY + NQ - 2)
    send_y(lambda to: send_l.at[to], got_l, 0)
    for load in loads[3:]:
        load.wait()
    wr = jnp.concatenate([mm(wr_ref[:, :128], by_q), mm(wr_ref[:, 128:], by_q)], axis=1).astype(BF16)
    right = edge(wr)
    right = jnp.stack([right[:, :256].reshape(NQ, 8, 256), right[:, 256:].reshape(NQ, 8, 256)], axis=1)
    send_r[...] = right.reshape(NQ, 16, 256).astype(BF16)
    send_q(lambda to: send_r.at[to], got_r, 1)
    got_l[y] = send_l[y]
    got_r[q] = send_r[q]

    rows0 = jnp.where(lane % 2 == 0, maskf[0:1, :128], maskf[0:1, 128:])
    rows1 = jnp.where(lane % 2 == 0, maskf[1:2, :128], maskf[1:2, 128:])
    eye = onehot(lane == col)
    spread = jnp.where(lane < 64, rows0, rows1).astype(BF16)
    send_m[...] = mm(eye, spread, NT).astype(BF16).reshape(NY, 16, 128)
    send_y(lambda to: pair_in.at[:, :, to], got_p, 2)
    send_y(lambda to: send_m.at[to], got_m, 3)
    got_p[y] = pair_ref[:, :, y]
    got_m[y] = send_m[y]

    r, s = grid_of(256, 256)
    turn = onehot((r // 16 == s % 16) & ((r // 8) % 2 == (s // 16) % 2) & (r % 8 == s // 32))
    split = onehot((r % 2 == (s // 8) % 2) & ((r // 2) % 16 == s // 16) & (r // 32 == s % 8))
    twice = onehot(lax.broadcasted_iota(jnp.int32, (512, 256), 0) // 2 == lax.broadcasted_iota(jnp.int32, (512, 256), 1))
    even = lax.broadcasted_iota(jnp.int32, (512, 128), 0) % 2 == 0
    gather = onehot((s % 4 == r // 64) & (s // 4 == r % 64))

    arrive(1)
    next_r[...] = mm(split, got_r[...].reshape(256, 256)).astype(BF16).reshape(NY, 32, 256)
    send_y(lambda to: next_r.at[to], have_r, 5)
    arrive(0)
    next_l[...] = mm(turn, got_l[...].reshape(256, 256)).astype(BF16).reshape(NQ, 16, 256)
    send_q(lambda to: next_l.at[to], have_l, 4)
    have_l[q] = next_l[q]
    have_r[y] = next_r[y]

    arrive(2)
    arrive(3)
    m0 = got_m[...].astype(F32)
    m1 = pltpu.roll(m0.reshape(128, 128), 64, 1).reshape(NY, 16, 128)
    m01 = jnp.stack([m0, m1], axis=1).reshape(256, 128).astype(BF16)
    m01 = mm(turn, m01).astype(BF16).reshape(8, 2, 16, 128)
    for z in range(2):
        part = mm(turn, got_p[:, :, z].reshape(256, 128)).astype(BF16)
        next_p[z * 8 : z * 8 + 8, 0:2] = part.reshape(8, 2, 16, 128)
        next_p[z * 8 : z * 8 + 8, 2:4] = m01
    send_q(lambda to: next_p.at[to], have_p, 6)
    have_p[q] = next_p[q]

    arrive(5)
    doubled = mm(twice, have_r[...].reshape(256, 256)).astype(BF16)
    arrive(4)
    tri = mm(doubled, have_l[...].reshape(256, 256), NT)
    tri = jnp.where(even, tri[:, :128], tri[:, 128:])
    send_t[...] = tri.reshape(128, 4, 128).astype(BF16)
    sent[7] = due[7] = have_t.at[pl.ds(0, 127)]
    place = y * 16 + q
    for step in FAR_ALL:
        to, part = at_q[step[0], step[2], step[3]]
        send(send_t.at[y_slot[step[1]] + to], have_t.at[place], 7, part + y_part[step[1]])
    have_t[place] = send_t[place]

    arrive(6)
    pairs, gates, lives = [], [], []
    pick = onehot(lane == zl)
    for jj in range(2):
        p = have_p[:, jj].reshape(256, 128).astype(F32)
        zc = norm(p, 1).astype(BF16)
        pairs.append(p)
        gates.append(jax.nn.sigmoid(mm(zc, wg_ref[...])))
        lives.append(mm(have_p[:, 2 + jj].reshape(256, 128), pick))
    wa = wa_ref[...]
    wk = wa[:, 128:256]
    wq_t, wv_t, wgate_t = wa[:, :128], wa[:, 256:384], wa[:, 384:]

    order = onehot(
        (s // 128 == (r // 16) % 2)
        & ((s // 16) % 8 == r % 8)
        & ((s // 8) % 2 == r // 128)
        & ((s // 4) % 2 == (r // 8) % 2)
        & (s % 4 == (r // 32) % 4)
    )
    arrive(7)

    pair1, yns = [], []
    tris = [mm(gather, have_t[b * 64 : b * 64 + 64].reshape(256, 128)).reshape(4, 64, 128) for b in range(2)]
    for jj in range(2):
        t = jnp.concatenate(
            [jnp.concatenate([tris[b][jj * 2 + half] for b in range(2)], axis=0) for half in range(2)], axis=1
        )
        tn = norm(t, 0).astype(BF16)
        p1 = pairs[jj] + gates[jj] * mm(tn, wo_ref[...], YN)
        pair1.append(p1)
        yns.append(norm(p1, 1).astype(BF16))

    parts = [mm(wb_ref[...], yn, NT) for yn in yns]
    both = jnp.concatenate(parts, axis=0)
    send_b[...] = jnp.concatenate([both[:, :128], both[:, 128:]], axis=0).astype(BF16)
    chip, core = q // 2, q % 2
    for step in FAR_ALL:
        if step[3] == 0:
            send(send_b, have_b.at[chip, core, y], 9 + step[1], at_q[step[0], step[2], 0][1] + y_part[step[1]])
    have_b[chip, core, y] = send_b[...]
    for k in range(NY):
        sent[9 + k] = have_b.at[pl.ds(0, 8 if k else 7), 0, 0]

    keys, queries, values, out_gates = [], [], [], []
    for jj in range(2):
        keys.append(mm(yns[jj], wk).astype(BF16))
        queries.append(mm(wq_t, yns[jj], TT).astype(BF16))
        values.append(mm(wv_t, yns[jj], TT).astype(BF16))
        out_gates.append(jax.nn.sigmoid(mm(wgate_t, yns[jj], TT)))

    head_row = lax.broadcasted_iota(jnp.int32, (128, 256), 0) // 32
    scale = F32(32.0**-0.5)
    for jj in range(2):
        for h in range(4):
            qh = jnp.where(head_row == h, queries[jj].astype(F32), F32(0)).astype(BF16)
            scores[jj, h] = mm(keys[jj], qh) * scale

    sent[17] = due[17] = have_b.at[:, 0]
    for k in (0, 1, 7, 2, 6, 3, 5, 4):
        wait_on(sent[9 + k], rsem.at[9 + k])
        block = have_b.at[:, core, (y + NY - k) % NY]
        send(block, block, 17, device_of(near, y))
    arrive(17)
    biases = [mm(order, have_b[b].reshape(256, 128)).astype(BF16).reshape(8, 32, 128) for b in range(8)]
    atts = [[], []]
    ones = jnp.ones((16, 256), BF16)
    for h in range(4):
        bias = jnp.concatenate(
            [mm(eye, jnp.concatenate([b[kh * 4 + h] for b in biases], axis=0), NT) for kh in range(2)], axis=0
        )
        for jj in range(2):
            live = jnp.concatenate([lives[jj], lives[jj]], axis=1) > 0.5
            sc = jnp.where(live, scores[jj, h] + bias, F32(-1e9))
            e = jnp.exp(sc - jnp.max(sc, axis=0, keepdims=True))
            o = mm(jnp.concatenate([values[jj][h * 32 : (h + 1) * 32], ones], axis=0), e.astype(BF16))
            atts[jj].append(out_gates[jj][h * 32 : (h + 1) * 32] * (o[:32] / o[32:33]))
    for jj in range(2):
        att = jnp.concatenate(atts[jj], axis=0).astype(BF16)
        res = pair1[jj] + mm(att, wao_ref[...], YN)
        for qq in range(NQ):
            for ii in range(2):
                start = (qq // 8) * 256 + (qq % 8) * 4 + ii * 2 + jj
                out_ref[pl.ds(start, 8, stride=32), :] = res[qq * 16 + ii * 8 : qq * 16 + ii * 8 + 8]

    for k, ref in sent.items():
        wait_on(ref, ssem.at[k])


def shards(pair, pair_mask, wl, wr, wg, wo, wa, wb, wao):
    vm = pl.BlockSpec(memory_space=pltpu.VMEM)
    hbm = pl.BlockSpec(memory_space=pltpu.HBM)
    inputs = (pair.reshape(2, 2, 8, 16, 128), pair_mask, wl, wr, wg, wo, wa, wb.T, wao)
    out = pl.pallas_call(
        kernel,
        out_shape=jax.ShapeDtypeStruct((512, 128), F32),
        in_specs=[hbm] * 9,
        out_specs=vm,
        scratch_shapes=[
            pltpu.VMEM((2, 2, 8, 16, 128), BF16),
            pltpu.VMEM((2, 256), jnp.int32),
            pltpu.VMEM((128, 256), BF16),
            pltpu.VMEM((128, 256), BF16),
            pltpu.VMEM((128, 128), BF16),
            pltpu.VMEM((128, 128), BF16),
            pltpu.VMEM((128, 512), BF16),
            pltpu.VMEM((4, 128), BF16),
            pltpu.VMEM((128, 128), BF16),
            pltpu.VMEM((NY, 2, 16, 256), BF16),
            pltpu.VMEM((NQ, 16, 256), BF16),
            pltpu.VMEM((NY, 16, 128), BF16),
            pltpu.VMEM((NY, 2, 16, 256), BF16),
            pltpu.VMEM((NQ, 16, 256), BF16),
            pltpu.VMEM((NY, 2, 2, 16, 128), BF16),
            pltpu.VMEM((NY, 16, 128), BF16),
            pltpu.VMEM((NQ, 16, 256), BF16),
            pltpu.VMEM((NY, 32, 256), BF16),
            pltpu.VMEM((NQ, 4, 16, 128), BF16),
            pltpu.VMEM((NQ, 16, 256), BF16),
            pltpu.VMEM((NY, 32, 256), BF16),
            pltpu.VMEM((NQ, 4, 16, 128), BF16),
            pltpu.VMEM((128, 4, 128), BF16),
            pltpu.VMEM((128, 4, 128), BF16),
            pltpu.VMEM((16, 128), BF16),
            pltpu.VMEM((8, 2, NY, 16, 128), BF16),
            pltpu.VMEM((2, 4, 256, 256), F32),
            pltpu.SemaphoreType.DMA((18,)),
            pltpu.SemaphoreType.DMA((18,)),
            pltpu.SemaphoreType.DMA((9,)),
        ],
        compiler_params=pltpu.CompilerParams(
            collective_id=0, has_side_effects=True, vmem_limit_bytes=32 * 1024 * 1024
        ),
    )(*(pltpu.with_memory_space_constraint(a, pltpu.HBM) for a in inputs))
    return out.reshape(256, 2, 128)


def solution(mesh):
    rows = ("dp", "dap")
    return jax.shard_map(
        shards,
        mesh=mesh,
        in_specs=(P(rows, None, None), P(rows, None), P(), P(), P(), P(), P(), P(), P()),
        out_specs=P("dp", "dap", None),
        check_vma=False,
    )
```

```python
import itertools

import jax
import jax.numpy as jnp
from jax import lax
from jax.experimental import pallas as pl
from jax.experimental.pallas import tpu as pltpu
from jax.sharding import PartitionSpec as P

MESH = pl.DeviceIdType.MESH
BF16 = jnp.bfloat16
F32 = jnp.float32
NY = 8
NQ = 16
YN = (((0,), (0,)), ((), ()))
NT = (((1,), (1,)), ((), ()))
TT = (((0,), (1,)), ((), ()))


FAR_Y = (4, 3, 5, 2, 6, 1, 7)
FAR_Q = tuple((dz, dx, dc) for dz, dx in ((1, 2), (1, 1), (1, 3), (0, 2), (0, 1), (0, 3), (1, 0)) for dc in (0, 1)) + ((0, 0, 1),)
FAR_ALL = tuple(
    sorted(
        (s for s in itertools.product(range(2), range(8), range(4), range(2)) if any(s)),
        key=lambda s: -(s[0] + min(s[1], 8 - s[1]) + min(s[2], 4 - s[2]) + 0.1 * s[3]),
    )
)


def natural(q):
    return (q // 4) % 2 * 8 + q % 4 * 2 + q // 8


def mm(a, b, dims=(((1,), (0,)), ((), ()))):
    return lax.dot_general(a, b, dims, preferred_element_type=F32)


def norm(x, axis):
    mean = jnp.mean(x, axis=axis, keepdims=True)
    d = x - mean
    var = jnp.mean(d * d, axis=axis, keepdims=True)
    return d * lax.rsqrt(var + 1e-05)


def grid_of(n, m):
    return (
        lax.broadcasted_iota(jnp.int32, (n, m), 0),
        lax.broadcasted_iota(jnp.int32, (n, m), 1),
    )


def onehot(cond):
    return jnp.where(cond, F32(1), F32(0)).astype(BF16)


def kernel(
    pair_in, mask_in, wl_in, wr_in, wg_in, wo_in, wa_in, wb_in, wao_in, out_ref,
    pair_ref, mask_ref, wl_ref, wr_ref, wg_ref, wo_ref, wa_ref, wb_ref, wao_ref,
    send_l, send_r, send_m, got_l, got_r, got_p, got_m,
    next_l, next_r, next_p, have_l, have_r, have_p,
    send_t, have_t, send_b, have_b, scores, pair1, out_gates, ssem, rsem, lsem,
):
    me = lax.axis_index("dap")
    zl, y, x_at, core = me // 64, (me // 8) % 8, (me // 2) % 4, me % 2
    q = core * 8 + zl * 4 + x_at
    at_y = [(y + s) % NY for s in range(NY)]
    at_q = {}
    for dz, dx, dc in itertools.product(range(2), range(4), range(2)):
        z, xx, cc = (zl + dz) % 2, (x_at + dx) % 4, (core + dc) % 2
        at_q[dz, dx, dc] = (cc * 8 + z * 4 + xx, z * 64 + xx * 2 + cc)
    y_part = [v * 8 for v in at_y]
    y_slot = [v * 16 for v in at_y]

    loads = [
        pltpu.make_async_copy(a, b, lsem.at[k])
        for k, (a, b) in enumerate((
            (pair_in, pair_ref), (wl_in, wl_ref), (mask_in, mask_ref), (wr_in, wr_ref), (wg_in, wg_ref),
            (wo_in, wo_ref), (wa_in, wa_ref), (wb_in, wb_ref), (wao_in, wao_ref),
        ))
    ]
    for load in loads:
        load.start()
    barrier = pltpu.get_barrier_semaphore()

    own = at_q[0, 0, 0][1]
    peers = [own + y_part[s] for s in FAR_Y] + [at_q[step][1] + y_part[0] for step in FAR_Q]
    for peer in peers:
        pl.semaphore_signal(barrier, inc=1, device_id={"dap": peer}, device_id_type=MESH)

    sent, due = {}, {}
    near = at_q[0, 0, 1][1] + y_part[0]

    def send(src, dst, k, peer):
        pltpu.make_async_remote_copy(
            src_ref=src, dst_ref=dst, send_sem=ssem.at[k], recv_sem=rsem.at[k],
            device_id={"dap": peer}, device_id_type=MESH,
        ).start()

    def send_y(src, dst, k):
        sent[k] = due[k] = dst.at[pl.ds(0, NY - 1)]
        for s in FAR_Y:
            send(src(at_y[s]), dst.at[y], k, own + y_part[s])

    def send_q(src, dst, k):
        sent[k] = due[k] = dst.at[pl.ds(0, NQ - 1)]
        for step in FAR_Q:
            to, part = at_q[step]
            send(src(to), dst.at[q], k, part + y_part[0])

    def wait_on(ref, sem):
        pltpu.make_async_copy(ref, ref, sem).wait()

    def arrive(k):
        wait_on(due.pop(k), rsem.at[k])

    for load in loads[:3]:
        load.wait()
    x = pair_ref[...].astype(F32).reshape(512, 128)
    zn = norm(x, 1).astype(BF16)
    maskf = mask_ref[...].astype(F32)
    mask_row = jnp.concatenate([maskf[0:1], maskf[1:2]], axis=1)

    lane, col = grid_of(128, 128)
    by_q = onehot((lane % 16 == col // 8) & (lane // 16 == col % 8))

    def edge(w):
        both = mm(w, zn, TT)
        return jax.nn.sigmoid(both[:128]) * both[128:] * mask_row

    left = edge(wl_ref[...]).astype(BF16)
    for ii in range(2):
        send_l[:, ii] = left[:, ii * 256 : (ii + 1) * 256].reshape(NY, 16, 256)
    pl.semaphore_wait(barrier, NY + NQ - 2)
    send_y(lambda to: send_l.at[to], got_l, 0)
    for load in loads[3:]:
        load.wait()
    wr = jnp.concatenate([mm(wr_ref[:, :128], by_q), mm(wr_ref[:, 128:], by_q)], axis=1).astype(BF16)
    right = edge(wr)
    right = jnp.stack([right[:, :256].reshape(NQ, 8, 256), right[:, 256:].reshape(NQ, 8, 256)], axis=1)
    send_r[...] = right.reshape(NQ, 16, 256).astype(BF16)
    send_q(lambda to: send_r.at[to], got_r, 1)
    got_l[y] = send_l[y]
    got_r[q] = send_r[q]

    rows0 = jnp.where(lane % 2 == 0, maskf[0:1, :128], maskf[0:1, 128:])
    rows1 = jnp.where(lane % 2 == 0, maskf[1:2, :128], maskf[1:2, 128:])
    eye = onehot(lane == col)
    spread = jnp.where(lane < 64, rows0, rows1).astype(BF16)
    send_m[...] = mm(eye, spread, NT).astype(BF16).reshape(NY, 16, 128)
    send_y(lambda to: pair_in.at[:, :, to], got_p, 2)
    send_y(lambda to: send_m.at[to], got_m, 3)
    got_p[y] = pair_ref[:, :, y]
    got_m[y] = send_m[y]

    r, s = grid_of(256, 256)
    turn = onehot((r // 16 == s % 16) & ((r // 8) % 2 == (s // 16) % 2) & (r % 8 == s // 32))
    split = onehot((r % 2 == (s // 8) % 2) & ((r // 2) % 16 == s // 16) & (r // 32 == s % 8))
    twice = onehot(lax.broadcasted_iota(jnp.int32, (512, 256), 0) // 2 == lax.broadcasted_iota(jnp.int32, (512, 256), 1))
    even = lax.broadcasted_iota(jnp.int32, (512, 128), 0) % 2 == 0
    gather = onehot((s % 4 == r // 64) & (s // 4 == r % 64))

    arrive(1)
    next_r[...] = mm(split, got_r[...].reshape(256, 256)).astype(BF16).reshape(NY, 32, 256)
    send_y(lambda to: next_r.at[to], have_r, 5)
    arrive(0)
    next_l[...] = mm(turn, got_l[...].reshape(256, 256)).astype(BF16).reshape(NQ, 16, 256)
    send_q(lambda to: next_l.at[to], have_l, 4)
    have_l[q] = next_l[q]
    have_r[y] = next_r[y]

    arrive(2)
    arrive(3)
    m0 = got_m[...].astype(F32)
    m1 = pltpu.roll(m0.reshape(128, 128), 64, 1).reshape(NY, 16, 128)
    m01 = jnp.stack([m0, m1], axis=1).reshape(256, 128).astype(BF16)
    m01 = mm(turn, m01).astype(BF16).reshape(8, 2, 16, 128)
    for z in range(2):
        part = mm(turn, got_p[:, :, z].reshape(256, 128)).astype(BF16)
        next_p[z * 8 : z * 8 + 8, 0:2] = part.reshape(8, 2, 16, 128)
        next_p[z * 8 : z * 8 + 8, 2:4] = m01
    send_q(lambda to: next_p.at[natural(to)], have_p, 6)
    have_p[q] = next_p[natural(q)]

    arrive(5)
    doubled = mm(twice, have_r[...].reshape(256, 256)).astype(BF16)
    arrive(4)
    tri = mm(doubled, have_l[...].reshape(256, 256), NT)
    tri = jnp.where(even, tri[:, :128], tri[:, 128:])
    send_t[...] = tri.reshape(128, 4, 128).astype(BF16)
    sent[7] = due[7] = have_t.at[pl.ds(0, 127)]
    place = y * 16 + q
    for step in FAR_ALL:
        to, part = at_q[step[0], step[2], step[3]]
        send(send_t.at[y_slot[step[1]] + to], have_t.at[place], 7, part + y_part[step[1]])
    have_t[place] = send_t[place]

    arrive(6)
    pairs, gates, lives = [], [], []
    pick = onehot(lane == zl)
    for jj in range(2):
        p = have_p[:, jj].reshape(256, 128).astype(F32)
        zc = norm(p, 1).astype(BF16)
        pairs.append(p)
        gates.append(jax.nn.sigmoid(mm(zc, wg_ref[...])))
        lives.append(mm(have_p[:, 2 + jj].reshape(256, 128), pick))
    wa = wa_ref[...]
    wk = wa[:, 128:256]
    wq_t, wv_t, wgate_t = wa[:, :128], wa[:, 256:384], wa[:, 384:]

    order = onehot(
        (s // 128 == (r // 16) % 2)
        & ((s // 16) % 8 == r % 8)
        & ((s // 8) % 2 == r // 128)
        & ((s // 4) % 2 == (r // 8) % 2)
        & (s % 4 == (r // 32) % 4)
    )
    arrive(7)

    yns = []
    tris = [mm(gather, have_t[b * 64 : b * 64 + 64].reshape(256, 128)).reshape(4, 64, 128) for b in range(2)]
    for jj in range(2):
        t = jnp.concatenate(
            [jnp.concatenate([tris[b][jj * 2 + half] for b in range(2)], axis=0) for half in range(2)], axis=1
        )
        tn = norm(t, 0).astype(BF16)
        p1 = pairs[jj] + gates[jj] * mm(tn, wo_ref[...], YN)
        pair1[jj] = p1.reshape(2, 128, 128)
        yns.append(norm(p1, 1).astype(BF16))

    parts = [mm(wb_ref[...], yn, NT) for yn in yns]
    both = jnp.concatenate(parts, axis=0)
    send_b[...] = jnp.concatenate([both[:, :128], both[:, 128:]], axis=0).astype(BF16)
    chip = q % 8
    for step in FAR_ALL:
        if step[3] == 0:
            send(send_b, have_b.at[core, chip, y], 9 + step[1], at_q[step[0], step[2], 0][1] + y_part[step[1]])
    have_b[core, chip, y] = send_b[...]
    for k in range(NY):
        sent[9 + k] = have_b.at[0, pl.ds(0, 8 if k else 7), 0]

    keys, queries, values = [], [], []
    for jj in range(2):
        keys.append(mm(yns[jj], wk).astype(BF16))
        queries.append(mm(wq_t, yns[jj], TT).astype(BF16))
        values.append(mm(wv_t, yns[jj], TT).astype(BF16))
        gate = jax.nn.sigmoid(mm(wgate_t, yns[jj], TT))
        for half in range(2):
            out_gates[jj, half] = gate[:, half * 128 : half * 128 + 128]

    head_row = lax.broadcasted_iota(jnp.int32, (128, 256), 0) // 32
    scale = F32(32.0**-0.5)
    for jj in range(2):
        for h in range(4):
            qh = jnp.where(head_row == h, queries[jj].astype(F32), F32(0)).astype(BF16)
            score = mm(keys[jj], qh) * scale
            for half in range(2):
                scores[jj, h, half] = score[:, half * 128 : half * 128 + 128]

    sent[17] = due[17] = have_b.at[0]
    for k in (0, 1, 7, 2, 6, 3, 5, 4):
        wait_on(sent[9 + k], rsem.at[9 + k])
        block = have_b.at[core, :, (y + NY - k) % NY]
        send(block, block, 17, near)

    ones = jnp.ones((16, 256), BF16)

    def finish(half):
        biases = [
            mm(order, have_b[half, 2 * b : 2 * b + 2].reshape(256, 128)).astype(BF16).reshape(8, 32, 128) for b in range(4)
        ]
        atts = [[], []]
        for h in range(4):
            bias = jnp.concatenate(
                [mm(eye, jnp.concatenate([b[kh * 4 + h] for b in biases], axis=0), NT) for kh in range(2)], axis=0
            )
            for jj in range(2):
                sc = jnp.where(lives[jj] > 0.5, scores[jj, h, half] + bias, F32(-1e9))
                e = jnp.exp(sc - jnp.max(sc, axis=0, keepdims=True))
                o = mm(jnp.concatenate([values[jj][h * 32 : (h + 1) * 32], ones], axis=0), e.astype(BF16))
                atts[jj].append(o[:32] / o[32:33])
        for jj in range(2):
            att = (jnp.concatenate(atts[jj], axis=0) * out_gates[jj, half]).astype(BF16)
            res = pair1[jj, half] + mm(att, wao_ref[...], YN)
            for k in range(8):
                for ii in range(2):
                    start = (k // 4) * 256 + (k % 4 * 2 + half) * 4 + ii * 2 + jj
                    out_ref[pl.ds(start, 8, stride=32), :] = res[k * 16 + ii * 8 : k * 16 + ii * 8 + 8]

    finish(core)
    arrive(17)
    finish(1 - core)

    for k, ref in sent.items():
        wait_on(ref, ssem.at[k])


def shards(pair, pair_mask, wl, wr, wg, wo, wa, wb, wao):
    vm = pl.BlockSpec(memory_space=pltpu.VMEM)
    hbm = pl.BlockSpec(memory_space=pltpu.HBM)
    inputs = (pair.reshape(2, 2, 8, 16, 128), pair_mask, wl, wr, wg, wo, wa, wb.T, wao)
    out = pl.pallas_call(
        kernel,
        out_shape=jax.ShapeDtypeStruct((512, 128), F32),
        in_specs=[hbm] * 9,
        out_specs=vm,
        scratch_shapes=[
            pltpu.VMEM((2, 2, 8, 16, 128), BF16),
            pltpu.VMEM((2, 256), jnp.int32),
            pltpu.VMEM((128, 256), BF16),
            pltpu.VMEM((128, 256), BF16),
            pltpu.VMEM((128, 128), BF16),
            pltpu.VMEM((128, 128), BF16),
            pltpu.VMEM((128, 512), BF16),
            pltpu.VMEM((4, 128), BF16),
            pltpu.VMEM((128, 128), BF16),
            pltpu.VMEM((NY, 2, 16, 256), BF16),
            pltpu.VMEM((NQ, 16, 256), BF16),
            pltpu.VMEM((NY, 16, 128), BF16),
            pltpu.VMEM((NY, 2, 16, 256), BF16),
            pltpu.VMEM((NQ, 16, 256), BF16),
            pltpu.VMEM((NY, 2, 2, 16, 128), BF16),
            pltpu.VMEM((NY, 16, 128), BF16),
            pltpu.VMEM((NQ, 16, 256), BF16),
            pltpu.VMEM((NY, 32, 256), BF16),
            pltpu.VMEM((NQ, 4, 16, 128), BF16),
            pltpu.VMEM((NQ, 16, 256), BF16),
            pltpu.VMEM((NY, 32, 256), BF16),
            pltpu.VMEM((NQ, 4, 16, 128), BF16),
            pltpu.VMEM((128, 4, 128), BF16),
            pltpu.VMEM((128, 4, 128), BF16),
            pltpu.VMEM((16, 128), BF16),
            pltpu.VMEM((2, 8, NY, 16, 128), BF16),
            pltpu.VMEM((2, 4, 2, 256, 128), F32),
            pltpu.VMEM((2, 2, 128, 128), F32),
            pltpu.VMEM((2, 2, 128, 128), F32),
            pltpu.SemaphoreType.DMA((18,)),
            pltpu.SemaphoreType.DMA((18,)),
            pltpu.SemaphoreType.DMA((9,)),
        ],
        compiler_params=pltpu.CompilerParams(
            collective_id=0, has_side_effects=True, vmem_limit_bytes=32 * 1024 * 1024
        ),
    )(*(pltpu.with_memory_space_constraint(a, pltpu.HBM) for a in inputs))
    return out.reshape(256, 2, 128)


def solution(mesh):
    rows = ("dp", "dap")
    return jax.shard_map(
        shards,
        mesh=mesh,
        in_specs=(P(rows, None, None), P(rows, None), P(), P(), P(), P(), P(), P(), P()),
        out_specs=P("dp", "dap", None),
        check_vma=False,
    )
```

```python
import itertools

import jax
import jax.numpy as jnp
from jax import lax
from jax.experimental import pallas as pl
from jax.experimental.pallas import tpu as pltpu
from jax.sharding import PartitionSpec as P

MESH = pl.DeviceIdType.MESH
BF16 = jnp.bfloat16
F32 = jnp.float32
NY = 8
NQ = 16
YN = (((0,), (0,)), ((), ()))
NT = (((1,), (1,)), ((), ()))
TT = (((0,), (1,)), ((), ()))


FAR_Y = (4, 3, 5, 2, 6, 1, 7)
FAR_Q = tuple((dz, dx, dc) for dz, dx in ((1, 2), (1, 1), (1, 3), (0, 2), (0, 1), (0, 3), (1, 0)) for dc in (0, 1)) + ((0, 0, 1),)
FAR_ALL = tuple(
    sorted(
        (s for s in itertools.product(range(2), range(8), range(4), range(2)) if any(s)),
        key=lambda s: -(s[0] + min(s[1], 8 - s[1]) + min(s[2], 4 - s[2]) + 0.1 * s[3]),
    )
)


def natural(q):
    return (q // 4) % 2 * 8 + q % 4 * 2 + q // 8


def mm(a, b, dims=(((1,), (0,)), ((), ()))):
    return lax.dot_general(a, b, dims, preferred_element_type=F32)


def norm(x, axis):
    mean = jnp.mean(x, axis=axis, keepdims=True)
    d = x - mean
    var = jnp.mean(d * d, axis=axis, keepdims=True)
    return d * lax.rsqrt(var + 1e-05)


def grid_of(n, m):
    return (
        lax.broadcasted_iota(jnp.int32, (n, m), 0),
        lax.broadcasted_iota(jnp.int32, (n, m), 1),
    )


def onehot(cond):
    return jnp.where(cond, F32(1), F32(0)).astype(BF16)


def kernel(
    pair_in, mask_in, wl_in, wr_in, wg_in, wo_in, wa_in, wb_in, wao_in, out_ref,
    pair_ref, mask_ref, wl_ref, wr_ref, wg_ref, wo_ref, wa_ref, wb_ref, wao_ref,
    send_l, send_r, send_m, got_l, got_r, got_p, got_m,
    next_l, next_r, next_p, have_l, have_r, have_p,
    send_t, have_t, send_b, have_b, scores, pair1, out_gates, ssem, rsem, lsem,
):
    me = lax.axis_index("dap")
    zl, y, x_at, core = me // 64, (me // 8) % 8, (me // 2) % 4, me % 2
    q = core * 8 + zl * 4 + x_at
    at_y = [(y + s) % NY for s in range(NY)]
    at_q = {}
    for dz, dx, dc in itertools.product(range(2), range(4), range(2)):
        z, xx, cc = (zl + dz) % 2, (x_at + dx) % 4, (core + dc) % 2
        at_q[dz, dx, dc] = (cc * 8 + z * 4 + xx, z * 64 + xx * 2 + cc)
    y_part = [v * 8 for v in at_y]
    y_slot = [v * 16 for v in at_y]

    loads = [
        pltpu.make_async_copy(a, b, lsem.at[k])
        for k, (a, b) in enumerate((
            (pair_in, pair_ref), (wl_in, wl_ref), (mask_in, mask_ref), (wr_in, wr_ref), (wg_in, wg_ref),
            (wo_in, wo_ref), (wa_in, wa_ref), (wb_in, wb_ref), (wao_in, wao_ref),
        ))
    ]
    for load in loads:
        load.start()
    barrier = pltpu.get_barrier_semaphore()

    own = at_q[0, 0, 0][1]
    peers = [own + y_part[s] for s in FAR_Y] + [at_q[step][1] + y_part[0] for step in FAR_Q]
    for peer in peers:
        pl.semaphore_signal(barrier, inc=1, device_id={"dap": peer}, device_id_type=MESH)

    sent, due = {}, {}
    near = at_q[0, 0, 1][1] + y_part[0]

    def send(src, dst, k, peer):
        pltpu.make_async_remote_copy(
            src_ref=src, dst_ref=dst, send_sem=ssem.at[k], recv_sem=rsem.at[k],
            device_id={"dap": peer}, device_id_type=MESH,
        ).start()

    def send_y(src, dst, k):
        sent[k] = due[k] = dst.at[pl.ds(0, NY - 1)]
        for s in FAR_Y:
            send(src(at_y[s]), dst.at[y], k, own + y_part[s])

    def send_q(src, dst, k):
        sent[k] = due[k] = dst.at[pl.ds(0, NQ - 1)]
        for step in FAR_Q:
            to, part = at_q[step]
            send(src(to), dst.at[q], k, part + y_part[0])

    def wait_on(ref, sem):
        pltpu.make_async_copy(ref, ref, sem).wait()

    def arrive(k):
        wait_on(due.pop(k), rsem.at[k])

    for load in loads[:3]:
        load.wait()
    x = pair_ref[...].astype(F32).reshape(512, 128)
    zn = norm(x, 1).astype(BF16)
    maskf = mask_ref[...].astype(F32)
    mask_row = jnp.concatenate([maskf[0:1], maskf[1:2]], axis=1)

    lane, col = grid_of(128, 128)
    by_q = onehot((lane % 16 == col // 8) & (lane // 16 == col % 8))

    def edge(w):
        both = mm(w, zn, TT)
        return jax.nn.sigmoid(both[:128]) * both[128:] * mask_row

    left = edge(wl_ref[...]).astype(BF16)
    for ii in range(2):
        send_l[:, ii] = left[:, ii * 256 : (ii + 1) * 256].reshape(NY, 16, 256)
    pl.semaphore_wait(barrier, NY + NQ - 2)
    send_y(lambda to: send_l.at[to], got_l, 0)
    for load in loads[3:]:
        load.wait()
    wr = jnp.concatenate([mm(wr_ref[:, :128], by_q), mm(wr_ref[:, 128:], by_q)], axis=1).astype(BF16)
    right = edge(wr)
    right = jnp.stack([right[:, :256].reshape(NQ, 8, 256), right[:, 256:].reshape(NQ, 8, 256)], axis=1)
    send_r[...] = right.reshape(NQ, 16, 256).astype(BF16)
    send_q(lambda to: send_r.at[to], got_r, 1)
    got_l[y] = send_l[y]
    got_r[q] = send_r[q]

    rows0 = jnp.where(lane % 2 == 0, maskf[0:1, :128], maskf[0:1, 128:])
    rows1 = jnp.where(lane % 2 == 0, maskf[1:2, :128], maskf[1:2, 128:])
    eye = onehot(lane == col)
    spread = jnp.where(lane < 64, rows0, rows1).astype(BF16)
    send_m[...] = mm(eye, spread, NT).astype(BF16).reshape(NY, 16, 128)
    send_y(lambda to: pair_in.at[:, :, to], got_p, 2)
    send_y(lambda to: send_m.at[to], got_m, 3)
    got_p[y] = pair_ref[:, :, y]
    got_m[y] = send_m[y]

    r, s = grid_of(256, 256)
    turn = onehot((r // 16 == s % 16) & ((r // 8) % 2 == (s // 16) % 2) & (r % 8 == s // 32))
    split = onehot((r % 2 == (s // 8) % 2) & ((r // 2) % 16 == s // 16) & (r // 32 == s % 8))
    twice = onehot(lax.broadcasted_iota(jnp.int32, (512, 256), 0) // 2 == lax.broadcasted_iota(jnp.int32, (512, 256), 1))
    even = lax.broadcasted_iota(jnp.int32, (512, 128), 0) % 2 == 0
    gather = onehot((s % 4 == r // 64) & (s // 4 == r % 64))

    arrive(1)
    next_r[...] = mm(split, got_r[...].reshape(256, 256)).astype(BF16).reshape(NY, 32, 256)
    send_y(lambda to: next_r.at[to], have_r, 5)
    arrive(0)
    next_l[...] = mm(turn, got_l[...].reshape(256, 256)).astype(BF16).reshape(NQ, 16, 256)
    send_q(lambda to: next_l.at[to], have_l, 4)
    have_l[q] = next_l[q]
    have_r[y] = next_r[y]

    arrive(2)
    arrive(3)
    m0 = got_m[...].astype(F32)
    m1 = pltpu.roll(m0.reshape(128, 128), 64, 1).reshape(NY, 16, 128)
    m01 = jnp.stack([m0, m1], axis=1).reshape(256, 128).astype(BF16)
    m01 = mm(turn, m01).astype(BF16).reshape(8, 2, 16, 128)
    for z in range(2):
        part = mm(turn, got_p[:, :, z].reshape(256, 128)).astype(BF16)
        next_p[z * 8 : z * 8 + 8, 0:2] = part.reshape(8, 2, 16, 128)
        next_p[z * 8 : z * 8 + 8, 2:4] = m01
    send_q(lambda to: next_p.at[natural(to)], have_p, 6)
    have_p[q] = next_p[natural(q)]

    arrive(5)
    doubled = mm(twice, have_r[...].reshape(256, 256)).astype(BF16)
    arrive(4)
    tri = mm(doubled, have_l[...].reshape(256, 256), NT)
    tri = jnp.where(even, tri[:, :128], tri[:, 128:])
    send_t[...] = tri.reshape(128, 4, 128).astype(BF16)
    sent[7] = due[7] = have_t.at[pl.ds(0, 127)]
    place = y * 16 + q
    for step in FAR_ALL:
        to, part = at_q[step[0], step[2], step[3]]
        send(send_t.at[y_slot[step[1]] + to], have_t.at[place], 7, part + y_part[step[1]])
    have_t[place] = send_t[place]

    arrive(6)
    pairs, gates, lives = [], [], []
    pick = onehot(lane == zl)
    for jj in range(2):
        p = mm(eye, have_p[:, jj].reshape(256, 128), NT)
        zc = norm(p, 0).astype(BF16)
        pairs.append(p)
        gates.append(jax.nn.sigmoid(mm(wg_ref[...], zc, YN)))
        lives.append(mm(have_p[:, 2 + jj].reshape(256, 128), pick))
    wa = wa_ref[...]
    wq_t, wk_t, wv_t, wgate_t, wo_t = (
        mm(eye, w, NT).astype(BF16) for w in (wa[:, :128], wa[:, 128:256], wa[:, 256:384], wa[:, 384:], wo_ref[...])
    )

    order = onehot(
        (s // 128 == (r // 16) % 2)
        & ((s // 16) % 8 == r % 8)
        & ((s // 8) % 2 == r // 128)
        & ((s // 4) % 2 == (r // 8) % 2)
        & (s % 4 == (r // 32) % 4)
    )
    arrive(7)

    p1s, yns = [], []
    tris = [mm(gather, have_t[b * 64 : b * 64 + 64].reshape(256, 128)).reshape(4, 64, 128) for b in range(2)]
    for jj in range(2):
        t = jnp.concatenate(
            [jnp.concatenate([tris[b][jj * 2 + half] for b in range(2)], axis=0) for half in range(2)], axis=1
        )
        tn = norm(t, 0).astype(BF16)
        p1 = pairs[jj] + gates[jj] * mm(wo_t, tn)
        p1s.append(p1)
        yns.append(norm(p1, 0).astype(BF16))

    parts = [mm(wb_ref[...], yn) for yn in yns]
    both = jnp.concatenate(parts, axis=0)
    send_b[...] = jnp.concatenate([both[:, :128], both[:, 128:]], axis=0).astype(BF16)
    chip = q % 8
    for step in FAR_ALL:
        if step[3] == 0:
            send(send_b, have_b.at[core, chip, y], 9 + step[1], at_q[step[0], step[2], 0][1] + y_part[step[1]])
    have_b[core, chip, y] = send_b[...]
    for k in range(NY):
        sent[9 + k] = have_b.at[0, pl.ds(0, 8 if k else 7), 0]

    keys, queries, values = [], [], []
    for jj in range(2):
        keys.append(mm(mm(wk_t, yns[jj]).astype(BF16), eye, YN).astype(BF16))
        queries.append(mm(wq_t, yns[jj]).astype(BF16))
        values.append(mm(wv_t, yns[jj]).astype(BF16))
        gate = jax.nn.sigmoid(mm(wgate_t, yns[jj]))
        for half in range(2):
            pair1[jj, half] = p1s[jj][:, half * 128 : half * 128 + 128].T
            out_gates[jj, half] = gate[:, half * 128 : half * 128 + 128]

    head_row = lax.broadcasted_iota(jnp.int32, (128, 256), 0) // 32
    scale = F32(32.0**-0.5)
    for jj in range(2):
        for h in range(4):
            qh = jnp.where(head_row == h, queries[jj].astype(F32), F32(0)).astype(BF16)
            score = mm(keys[jj], qh) * scale
            for half in range(2):
                scores[jj, h, half] = score[:, half * 128 : half * 128 + 128]

    sent[17] = due[17] = have_b.at[0]
    for k in (0, 1, 7, 2, 6, 3, 5, 4):
        wait_on(sent[9 + k], rsem.at[9 + k])
        block = have_b.at[core, :, (y + NY - k) % NY]
        send(block, block, 17, near)

    ones = jnp.ones((16, 256), BF16)

    def finish(half):
        biases = [
            mm(order, have_b[half, 2 * b : 2 * b + 2].reshape(256, 128)).astype(BF16).reshape(8, 32, 128) for b in range(4)
        ]
        atts = [[], []]
        for h in range(4):
            bias = jnp.concatenate(
                [mm(eye, jnp.concatenate([b[kh * 4 + h] for b in biases], axis=0), NT) for kh in range(2)], axis=0
            )
            for jj in range(2):
                sc = jnp.where(lives[jj] > 0.5, scores[jj, h, half] + bias, F32(-1e9))
                e = jnp.exp(sc - jnp.max(sc, axis=0, keepdims=True))
                o = mm(jnp.concatenate([values[jj][h * 32 : (h + 1) * 32], ones], axis=0), e.astype(BF16))
                atts[jj].append(o[:32] / o[32:33])
        for jj in range(2):
            att = (jnp.concatenate(atts[jj], axis=0) * out_gates[jj, half]).astype(BF16)
            res = pair1[jj, half] + mm(att, wao_ref[...], YN)
            for k in range(8):
                for ii in range(2):
                    start = (k // 4) * 256 + (k % 4 * 2 + half) * 4 + ii * 2 + jj
                    out_ref[pl.ds(start, 8, stride=32), :] = res[k * 16 + ii * 8 : k * 16 + ii * 8 + 8]

    finish(core)
    arrive(17)
    finish(1 - core)

    for k, ref in sent.items():
        wait_on(ref, ssem.at[k])


def shards(pair, pair_mask, wl, wr, wg, wo, wa, wb, wao):
    vm = pl.BlockSpec(memory_space=pltpu.VMEM)
    hbm = pl.BlockSpec(memory_space=pltpu.HBM)
    inputs = (pair.reshape(2, 2, 8, 16, 128), pair_mask, wl, wr, wg, wo, wa, wb.T, wao)
    out = pl.pallas_call(
        kernel,
        out_shape=jax.ShapeDtypeStruct((512, 128), F32),
        in_specs=[hbm] * 9,
        out_specs=vm,
        scratch_shapes=[
            pltpu.VMEM((2, 2, 8, 16, 128), BF16),
            pltpu.VMEM((2, 256), jnp.int32),
            pltpu.VMEM((128, 256), BF16),
            pltpu.VMEM((128, 256), BF16),
            pltpu.VMEM((128, 128), BF16),
            pltpu.VMEM((128, 128), BF16),
            pltpu.VMEM((128, 512), BF16),
            pltpu.VMEM((4, 128), BF16),
            pltpu.VMEM((128, 128), BF16),
            pltpu.VMEM((NY, 2, 16, 256), BF16),
            pltpu.VMEM((NQ, 16, 256), BF16),
            pltpu.VMEM((NY, 16, 128), BF16),
            pltpu.VMEM((NY, 2, 16, 256), BF16),
            pltpu.VMEM((NQ, 16, 256), BF16),
            pltpu.VMEM((NY, 2, 2, 16, 128), BF16),
            pltpu.VMEM((NY, 16, 128), BF16),
            pltpu.VMEM((NQ, 16, 256), BF16),
            pltpu.VMEM((NY, 32, 256), BF16),
            pltpu.VMEM((NQ, 4, 16, 128), BF16),
            pltpu.VMEM((NQ, 16, 256), BF16),
            pltpu.VMEM((NY, 32, 256), BF16),
            pltpu.VMEM((NQ, 4, 16, 128), BF16),
            pltpu.VMEM((128, 4, 128), BF16),
            pltpu.VMEM((128, 4, 128), BF16),
            pltpu.VMEM((16, 128), BF16),
            pltpu.VMEM((2, 8, NY, 16, 128), BF16),
            pltpu.VMEM((2, 4, 2, 256, 128), F32),
            pltpu.VMEM((2, 2, 128, 128), F32),
            pltpu.VMEM((2, 2, 128, 128), F32),
            pltpu.SemaphoreType.DMA((18,)),
            pltpu.SemaphoreType.DMA((18,)),
            pltpu.SemaphoreType.DMA((9,)),
        ],
        compiler_params=pltpu.CompilerParams(
            collective_id=0, has_side_effects=True, vmem_limit_bytes=32 * 1024 * 1024
        ),
    )(*(pltpu.with_memory_space_constraint(a, pltpu.HBM) for a in inputs))
    return out.reshape(256, 2, 128)


def solution(mesh):
    rows = ("dp", "dap")
    return jax.shard_map(
        shards,
        mesh=mesh,
        in_specs=(P(rows, None, None), P(rows, None), P(), P(), P(), P(), P(), P(), P()),
        out_specs=P("dp", "dap", None),
        check_vma=False,
    )
```

```python
import itertools

import jax
import jax.numpy as jnp
from jax import lax
from jax.experimental import pallas as pl
from jax.experimental.pallas import tpu as pltpu
from jax.sharding import PartitionSpec as P

MESH = pl.DeviceIdType.MESH
BF16 = jnp.bfloat16
F32 = jnp.float32
NY = 8
NQ = 16
YN = (((0,), (0,)), ((), ()))
NT = (((1,), (1,)), ((), ()))
TT = (((0,), (1,)), ((), ()))


FAR_Y = (4, 3, 5, 2, 6, 1, 7)
FAR_Q = tuple((dz, dx, dc) for dz, dx in ((1, 2), (1, 1), (1, 3), (0, 2), (0, 1), (0, 3), (1, 0)) for dc in (0, 1)) + ((0, 0, 1),)
FAR_ALL = tuple(
    sorted(
        (s for s in itertools.product(range(2), range(8), range(4), range(2)) if any(s)),
        key=lambda s: -(s[0] + min(s[1], 8 - s[1]) + min(s[2], 4 - s[2]) + 0.1 * s[3]),
    )
)


def natural(q):
    return (q // 4) % 2 * 8 + q % 4 * 2 + q // 8


def mm(a, b, dims=(((1,), (0,)), ((), ()))):
    return lax.dot_general(a, b, dims, preferred_element_type=F32)


def norm(x, axis):
    mean = jnp.mean(x, axis=axis, keepdims=True)
    d = x - mean
    var = jnp.mean(d * d, axis=axis, keepdims=True)
    return d * lax.rsqrt(var + 1e-05)


def grid_of(n, m):
    return (
        lax.broadcasted_iota(jnp.int32, (n, m), 0),
        lax.broadcasted_iota(jnp.int32, (n, m), 1),
    )


def onehot(cond):
    return jnp.where(cond, F32(1), F32(0)).astype(BF16)


def kernel(
    pair_in, mask_in, wl_in, wr_in, wg_in, wo_in, wa_in, wb_in, wao_in, out_ref,
    pair_ref, mask_ref, wl_ref, wr_ref, wg_ref, wo_ref, wa_ref, wb_ref, wao_ref,
    send_l, send_r, send_m, got_l, got_r, got_p, got_m,
    next_l, next_r, next_p, have_l, have_r, have_p,
    send_t, have_t, send_b, have_b, scores, pair1, out_gates, ssem, rsem, lsem,
):
    me = lax.axis_index("dap")
    zl, y, x_at, core = me // 64, (me // 8) % 8, (me // 2) % 4, me % 2
    q = core * 8 + zl * 4 + x_at
    at_y = [(y + s) % NY for s in range(NY)]
    at_q = {}
    for dz, dx, dc in itertools.product(range(2), range(4), range(2)):
        z, xx, cc = (zl + dz) % 2, (x_at + dx) % 4, (core + dc) % 2
        at_q[dz, dx, dc] = (cc * 8 + z * 4 + xx, z * 64 + xx * 2 + cc)
    y_part = [v * 8 for v in at_y]
    y_slot = [v * 16 for v in at_y]

    loads = [
        pltpu.make_async_copy(a, b, lsem.at[k])
        for k, (a, b) in enumerate((
            (pair_in, pair_ref), (wl_in, wl_ref), (mask_in, mask_ref), (wr_in, wr_ref), (wg_in, wg_ref),
            (wo_in, wo_ref), (wa_in, wa_ref), (wb_in, wb_ref), (wao_in, wao_ref),
        ))
    ]
    for load in loads:
        load.start()
    barrier = pltpu.get_barrier_semaphore()

    own = at_q[0, 0, 0][1]
    peers = [own + y_part[s] for s in FAR_Y] + [at_q[step][1] + y_part[0] for step in FAR_Q]
    for peer in peers:
        pl.semaphore_signal(barrier, inc=1, device_id={"dap": peer}, device_id_type=MESH)

    sent, due = {}, {}
    near = at_q[0, 0, 1][1] + y_part[0]

    def send(src, dst, k, peer):
        pltpu.make_async_remote_copy(
            src_ref=src, dst_ref=dst, send_sem=ssem.at[k], recv_sem=rsem.at[k],
            device_id={"dap": peer}, device_id_type=MESH,
        ).start()

    def send_y(src, dst, k):
        sent[k] = due[k] = dst.at[pl.ds(0, NY - 1)]
        for s in FAR_Y:
            send(src(at_y[s]), dst.at[y], k, own + y_part[s])

    def send_q(src, dst, k):
        sent[k] = due[k] = dst.at[pl.ds(0, NQ - 1)]
        for step in FAR_Q:
            to, part = at_q[step]
            send(src(to), dst.at[q], k, part + y_part[0])

    def wait_on(ref, sem):
        pltpu.make_async_copy(ref, ref, sem).wait()

    def arrive(k):
        wait_on(due.pop(k), rsem.at[k])

    for load in loads[:3]:
        load.wait()
    x = pair_ref[...].astype(F32).reshape(512, 128)
    zn = norm(x, 1).astype(BF16)
    maskf = mask_ref[...].astype(F32)
    mask_row = jnp.concatenate([maskf[0:1], maskf[1:2]], axis=1)

    lane, col = grid_of(128, 128)
    by_q = onehot((lane % 16 == col // 8) & (lane // 16 == col % 8))

    def edge(w):
        both = mm(w, zn, TT)
        return jax.nn.sigmoid(both[:128]) * both[128:] * mask_row

    left = edge(wl_ref[...]).astype(BF16)
    for ii in range(2):
        send_l[:, ii] = left[:, ii * 256 : (ii + 1) * 256].reshape(NY, 16, 256)
    pl.semaphore_wait(barrier, NY + NQ - 2)
    send_y(lambda to: send_l.at[to], got_l, 0)
    for load in loads[3:]:
        load.wait()
    wr = jnp.concatenate([mm(wr_ref[:, :128], by_q), mm(wr_ref[:, 128:], by_q)], axis=1).astype(BF16)
    right = edge(wr)
    right = jnp.stack([right[:, :256].reshape(NQ, 8, 256), right[:, 256:].reshape(NQ, 8, 256)], axis=1)
    send_r[...] = right.reshape(NQ, 16, 256).astype(BF16)
    send_q(lambda to: send_r.at[to], got_r, 1)
    got_l[y] = send_l[y]
    got_r[q] = send_r[q]

    rows0 = jnp.where(lane % 2 == 0, maskf[0:1, :128], maskf[0:1, 128:])
    rows1 = jnp.where(lane % 2 == 0, maskf[1:2, :128], maskf[1:2, 128:])
    eye = onehot(lane == col)
    spread = jnp.where(lane < 64, rows0, rows1).astype(BF16)
    send_m[...] = mm(eye, spread, NT).astype(BF16).reshape(NY, 16, 128)
    send_y(lambda to: pair_in.at[:, :, to], got_p, 2)
    send_y(lambda to: send_m.at[to], got_m, 3)
    got_p[y] = pair_ref[:, :, y]
    got_m[y] = send_m[y]

    r, s = grid_of(256, 256)
    turn = onehot((r // 16 == s % 16) & ((r // 8) % 2 == (s // 16) % 2) & (r % 8 == s // 32))
    split = onehot((r % 2 == (s // 8) % 2) & ((r // 2) % 16 == s // 16) & (r // 32 == s % 8))
    twice = onehot(lax.broadcasted_iota(jnp.int32, (512, 256), 0) // 2 == lax.broadcasted_iota(jnp.int32, (512, 256), 1))
    even = lax.broadcasted_iota(jnp.int32, (512, 128), 0) % 2 == 0
    gather = onehot((s % 4 == r // 64) & (s // 4 == r % 64))

    arrive(1)
    next_r[...] = mm(split, got_r[...].reshape(256, 256)).astype(BF16).reshape(NY, 32, 256)
    send_y(lambda to: next_r.at[to], have_r, 5)
    arrive(0)
    next_l[...] = mm(turn, got_l[...].reshape(256, 256)).astype(BF16).reshape(NQ, 16, 256)
    send_q(lambda to: next_l.at[to], have_l, 4)
    have_l[q] = next_l[q]
    have_r[y] = next_r[y]

    arrive(2)
    arrive(3)
    m0 = got_m[...].astype(F32)
    m1 = pltpu.roll(m0.reshape(128, 128), 64, 1).reshape(NY, 16, 128)
    m01 = jnp.stack([m0, m1], axis=1).reshape(256, 128).astype(BF16)
    m01 = mm(turn, m01).astype(BF16).reshape(8, 2, 16, 128)
    for z in range(2):
        part = mm(turn, got_p[:, :, z].reshape(256, 128)).astype(BF16)
        next_p[z * 8 : z * 8 + 8, 0:2] = part.reshape(8, 2, 16, 128)
        next_p[z * 8 : z * 8 + 8, 2:4] = m01
    send_q(lambda to: next_p.at[natural(to)], have_p, 6)
    have_p[q] = next_p[natural(q)]

    arrive(5)
    doubled = mm(twice, have_r[...].reshape(256, 256)).astype(BF16)
    arrive(4)
    tri = mm(doubled, have_l[...].reshape(256, 256), NT)
    tri = jnp.where(even, tri[:, :128], tri[:, 128:])
    send_t[...] = tri.reshape(128, 4, 128).astype(BF16)
    sent[7] = due[7] = have_t.at[pl.ds(0, 127)]
    place = y * 16 + q
    for step in FAR_ALL:
        to, part = at_q[step[0], step[2], step[3]]
        send(send_t.at[y_slot[step[1]] + to], have_t.at[place], 7, part + y_part[step[1]])
    have_t[place] = send_t[place]

    arrive(6)
    pairs, gates, lives = [], [], []
    pick = onehot(lane == zl)
    for jj in range(2):
        p = mm(eye, have_p[:, jj].reshape(256, 128), NT)
        zc = norm(p, 0).astype(BF16)
        pairs.append(p)
        gates.append(jax.nn.sigmoid(mm(wg_ref[...], zc, YN)))
        lives.append(mm(have_p[:, 2 + jj].reshape(256, 128), pick))
    wa = wa_ref[...]
    wq_t, wk_t, wv_t, wgate_t, wo_t = (
        mm(eye, w, NT).astype(BF16) for w in (wa[:, :128], wa[:, 128:256], wa[:, 256:384], wa[:, 384:], wo_ref[...])
    )

    order = onehot(
        (s // 128 == (r // 16) % 2)
        & ((s // 16) % 8 == r % 8)
        & ((s // 8) % 2 == r // 128)
        & ((s // 4) % 2 == (r // 8) % 2)
        & (s % 4 == (r // 32) % 4)
    )
    arrive(7)

    p1s, yns = [], []
    tris = [mm(gather, have_t[b * 64 : b * 64 + 64].reshape(256, 128)).reshape(4, 64, 128) for b in range(2)]
    for jj in range(2):
        t = jnp.concatenate(
            [jnp.concatenate([tris[b][jj * 2 + half] for b in range(2)], axis=0) for half in range(2)], axis=1
        )
        tn = norm(t, 0).astype(BF16)
        p1 = pairs[jj] + gates[jj] * mm(wo_t, tn)
        p1s.append(p1)
        yns.append(norm(p1, 0).astype(BF16))

    parts = [mm(wb_ref[...], yn) for yn in yns]
    both = jnp.concatenate(parts, axis=0)
    send_b[...] = jnp.concatenate([both[:, :128], both[:, 128:]], axis=0).astype(BF16)
    chip = q % 8
    for step in sorted(FAR_ALL, key=lambda v: (-(v[0] + 0.6 * min(v[1], 8 - v[1]) + 1.2 * min(v[2], 4 - v[2])), v)):
        if step[3] == 0:
            send(send_b, have_b.at[core, chip, y], 9 + step[1], at_q[step[0], step[2], 0][1] + y_part[step[1]])
    have_b[core, chip, y] = send_b[...]
    for k in range(NY):
        sent[9 + k] = have_b.at[0, pl.ds(0, 8 if k else 7), 0]

    keys, queries, values = [], [], []
    for jj in range(2):
        keys.append(mm(mm(wk_t, yns[jj]).astype(BF16), eye, YN).astype(BF16))
        queries.append(mm(wq_t, yns[jj]).astype(BF16))
        values.append(mm(wv_t, yns[jj]).astype(BF16))
        gate = jax.nn.sigmoid(mm(wgate_t, yns[jj]))
        for half in range(2):
            pair1[jj, half] = p1s[jj][:, half * 128 : half * 128 + 128].T
            out_gates[jj, half] = gate[:, half * 128 : half * 128 + 128]

    head_row = lax.broadcasted_iota(jnp.int32, (128, 256), 0) // 32
    scale = F32(32.0**-0.5)
    for jj in range(2):
        for h in range(4):
            qh = jnp.where(head_row == h, queries[jj].astype(F32), F32(0)).astype(BF16)
            score = mm(keys[jj], qh) * scale
            for half in range(2):
                scores[jj, h, half] = score[:, half * 128 : half * 128 + 128]

    sent[17] = due[17] = have_b.at[0]
    for k in (0, 1, 7, 2, 6, 3, 5, 4):
        wait_on(sent[9 + k], rsem.at[9 + k])
        block = have_b.at[core, :, (y + NY - k) % NY]
        send(block, block, 17, near)

    ones = jnp.ones((16, 256), BF16)

    def finish(half):
        biases = [
            mm(order, have_b[half, 2 * b : 2 * b + 2].reshape(256, 128)).astype(BF16).reshape(8, 32, 128) for b in range(4)
        ]
        atts = [[], []]
        for h in range(4):
            bias = jnp.concatenate(
                [mm(eye, jnp.concatenate([b[kh * 4 + h] for b in biases], axis=0), NT) for kh in range(2)], axis=0
            )
            for jj in range(2):
                sc = jnp.where(lives[jj] > 0.5, scores[jj, h, half] + bias, F32(-1e9))
                e = jnp.exp(sc - jnp.max(sc, axis=0, keepdims=True))
                o = mm(jnp.concatenate([values[jj][h * 32 : (h + 1) * 32], ones], axis=0), e.astype(BF16))
                atts[jj].append(o[:32] / o[32:33])
        for jj in range(2):
            att = (jnp.concatenate(atts[jj], axis=0) * out_gates[jj, half]).astype(BF16)
            res = pair1[jj, half] + mm(att, wao_ref[...], YN)
            for k in range(8):
                for ii in range(2):
                    start = (k // 4) * 256 + (k % 4 * 2 + half) * 4 + ii * 2 + jj
                    out_ref[pl.ds(start, 8, stride=32), :] = res[k * 16 + ii * 8 : k * 16 + ii * 8 + 8]

    finish(core)
    arrive(17)
    finish(1 - core)

    for k, ref in sent.items():
        wait_on(ref, ssem.at[k])


def shards(pair, pair_mask, wl, wr, wg, wo, wa, wb, wao):
    vm = pl.BlockSpec(memory_space=pltpu.VMEM)
    hbm = pl.BlockSpec(memory_space=pltpu.HBM)
    inputs = (pair.reshape(2, 2, 8, 16, 128), pair_mask, wl, wr, wg, wo, wa, wb.T, wao)
    out = pl.pallas_call(
        kernel,
        out_shape=jax.ShapeDtypeStruct((512, 128), F32),
        in_specs=[hbm] * 9,
        out_specs=vm,
        scratch_shapes=[
            pltpu.VMEM((2, 2, 8, 16, 128), BF16),
            pltpu.VMEM((2, 256), jnp.int32),
            pltpu.VMEM((128, 256), BF16),
            pltpu.VMEM((128, 256), BF16),
            pltpu.VMEM((128, 128), BF16),
            pltpu.VMEM((128, 128), BF16),
            pltpu.VMEM((128, 512), BF16),
            pltpu.VMEM((4, 128), BF16),
            pltpu.VMEM((128, 128), BF16),
            pltpu.VMEM((NY, 2, 16, 256), BF16),
            pltpu.VMEM((NQ, 16, 256), BF16),
            pltpu.VMEM((NY, 16, 128), BF16),
            pltpu.VMEM((NY, 2, 16, 256), BF16),
            pltpu.VMEM((NQ, 16, 256), BF16),
            pltpu.VMEM((NY, 2, 2, 16, 128), BF16),
            pltpu.VMEM((NY, 16, 128), BF16),
            pltpu.VMEM((NQ, 16, 256), BF16),
            pltpu.VMEM((NY, 32, 256), BF16),
            pltpu.VMEM((NQ, 4, 16, 128), BF16),
            pltpu.VMEM((NQ, 16, 256), BF16),
            pltpu.VMEM((NY, 32, 256), BF16),
            pltpu.VMEM((NQ, 4, 16, 128), BF16),
            pltpu.VMEM((128, 4, 128), BF16),
            pltpu.VMEM((128, 4, 128), BF16),
            pltpu.VMEM((16, 128), BF16),
            pltpu.VMEM((2, 8, NY, 16, 128), BF16),
            pltpu.VMEM((2, 4, 2, 256, 128), F32),
            pltpu.VMEM((2, 2, 128, 128), F32),
            pltpu.VMEM((2, 2, 128, 128), F32),
            pltpu.SemaphoreType.DMA((18,)),
            pltpu.SemaphoreType.DMA((18,)),
            pltpu.SemaphoreType.DMA((9,)),
        ],
        compiler_params=pltpu.CompilerParams(
            collective_id=0, has_side_effects=True, vmem_limit_bytes=32 * 1024 * 1024
        ),
    )(*(pltpu.with_memory_space_constraint(a, pltpu.HBM) for a in inputs))
    return out.reshape(256, 2, 128)


def solution(mesh):
    rows = ("dp", "dap")
    return jax.shard_map(
        shards,
        mesh=mesh,
        in_specs=(P(rows, None, None), P(rows, None), P(), P(), P(), P(), P(), P(), P()),
        out_specs=P("dp", "dap", None),
        check_vma=False,
    )
```

```python
import itertools

import jax
import jax.numpy as jnp
from jax import lax
from jax.experimental import pallas as pl
from jax.experimental.pallas import tpu as pltpu
from jax.sharding import PartitionSpec as P

MESH = pl.DeviceIdType.MESH
BF16 = jnp.bfloat16
F32 = jnp.float32
NY = 8
NQ = 16
YN = (((0,), (0,)), ((), ()))
NT = (((1,), (1,)), ((), ()))
TT = (((0,), (1,)), ((), ()))


FAR_Y = (4, 3, 5, 2, 6, 1, 7)
FAR_Q = tuple((dz, dx, dc) for dz, dx in ((1, 2), (1, 1), (1, 3), (0, 2), (0, 1), (0, 3), (1, 0)) for dc in (0, 1)) + ((0, 0, 1),)
FAR_ALL = tuple(
    sorted(
        (s for s in itertools.product(range(2), range(8), range(4), range(2)) if any(s)),
        key=lambda s: -(s[0] + 0.7 * min(s[1], 8 - s[1]) + min(s[2], 4 - s[2]) + 0.1 * s[3]),
    )
)


def natural(q):
    return (q // 4) % 2 * 8 + q % 4 * 2 + q // 8


def mm(a, b, dims=(((1,), (0,)), ((), ()))):
    return lax.dot_general(a, b, dims, preferred_element_type=F32)


def norm(x, axis):
    mean = jnp.mean(x, axis=axis, keepdims=True)
    d = x - mean
    var = jnp.mean(d * d, axis=axis, keepdims=True)
    return d * lax.rsqrt(var + 1e-05)


def grid_of(n, m):
    return (
        lax.broadcasted_iota(jnp.int32, (n, m), 0),
        lax.broadcasted_iota(jnp.int32, (n, m), 1),
    )


def onehot(cond):
    return jnp.where(cond, F32(1), F32(0)).astype(BF16)


def kernel(
    pair_in, mask_in, wl_in, wr_in, wg_in, wo_in, wa_in, wb_in, wao_in, out_ref,
    pair_ref, mask_ref, wl_ref, wr_ref, wg_ref, wo_ref, wa_ref, wb_ref, wao_ref,
    send_l, send_r, send_m, got_l, got_r, got_p, got_m,
    next_l, next_r, next_p, have_l, have_r, have_p,
    send_t, have_t, send_b, have_b, scores, pair1, out_gates, ssem, rsem, lsem,
):
    me = lax.axis_index("dap")
    zl, y, x_at, core = me // 64, (me // 8) % 8, (me // 2) % 4, me % 2
    q = core * 8 + zl * 4 + x_at
    at_y = [(y + s) % NY for s in range(NY)]
    at_q = {}
    for dz, dx, dc in itertools.product(range(2), range(4), range(2)):
        z, xx, cc = (zl + dz) % 2, (x_at + dx) % 4, (core + dc) % 2
        at_q[dz, dx, dc] = (cc * 8 + z * 4 + xx, z * 64 + xx * 2 + cc)
    y_part = [v * 8 for v in at_y]
    y_slot = [v * 16 for v in at_y]

    loads = [
        pltpu.make_async_copy(a, b, lsem.at[k])
        for k, (a, b) in enumerate((
            (pair_in, pair_ref), (wl_in, wl_ref), (mask_in, mask_ref), (wr_in, wr_ref), (wg_in, wg_ref),
            (wo_in, wo_ref), (wa_in, wa_ref), (wb_in, wb_ref), (wao_in, wao_ref),
        ))
    ]
    for load in loads:
        load.start()
    barrier = pltpu.get_barrier_semaphore()

    own = at_q[0, 0, 0][1]
    peers = [own + y_part[s] for s in FAR_Y] + [at_q[step][1] + y_part[0] for step in FAR_Q]
    for peer in peers:
        pl.semaphore_signal(barrier, inc=1, device_id={"dap": peer}, device_id_type=MESH)

    sent, due = {}, {}
    near = at_q[0, 0, 1][1] + y_part[0]

    def send(src, dst, k, peer):
        pltpu.make_async_remote_copy(
            src_ref=src, dst_ref=dst, send_sem=ssem.at[k], recv_sem=rsem.at[k],
            device_id={"dap": peer}, device_id_type=MESH,
        ).start()

    def send_y(src, dst, k):
        sent[k] = due[k] = dst.at[pl.ds(0, NY - 1)]
        for s in FAR_Y:
            send(src(at_y[s]), dst.at[y], k, own + y_part[s])

    def send_q(src, dst, k):
        sent[k] = due[k] = dst.at[pl.ds(0, NQ - 1)]
        for step in FAR_Q:
            to, part = at_q[step]
            send(src(to), dst.at[q], k, part + y_part[0])

    def wait_on(ref, sem):
        pltpu.make_async_copy(ref, ref, sem).wait()

    def arrive(k):
        wait_on(due.pop(k), rsem.at[k])

    for load in loads[:3]:
        load.wait()
    x = pair_ref[...].astype(F32).reshape(512, 128)
    zn = norm(x, 1).astype(BF16)
    maskf = mask_ref[...].astype(F32)
    mask_row = jnp.concatenate([maskf[0:1], maskf[1:2]], axis=1)

    lane, col = grid_of(128, 128)
    by_q = onehot((lane % 16 == col // 8) & (lane // 16 == col % 8))

    def edge(w):
        both = mm(w, zn, TT)
        return jax.nn.sigmoid(both[:128]) * both[128:] * mask_row

    left = edge(wl_ref[...]).astype(BF16)
    for ii in range(2):
        send_l[:, ii] = left[:, ii * 256 : (ii + 1) * 256].reshape(NY, 16, 256)
    pl.semaphore_wait(barrier, NY + NQ - 2)
    send_y(lambda to: send_l.at[to], got_l, 0)
    for load in loads[3:]:
        load.wait()
    wr = jnp.concatenate([mm(wr_ref[:, :128], by_q), mm(wr_ref[:, 128:], by_q)], axis=1).astype(BF16)
    right = edge(wr)
    right = jnp.stack([right[:, :256].reshape(NQ, 8, 256), right[:, 256:].reshape(NQ, 8, 256)], axis=1)
    send_r[...] = right.reshape(NQ, 16, 256).astype(BF16)
    send_q(lambda to: send_r.at[to], got_r, 1)
    got_l[y] = send_l[y]
    got_r[q] = send_r[q]

    rows0 = jnp.where(lane % 2 == 0, maskf[0:1, :128], maskf[0:1, 128:])
    rows1 = jnp.where(lane % 2 == 0, maskf[1:2, :128], maskf[1:2, 128:])
    eye = onehot(lane == col)
    spread = jnp.where(lane < 64, rows0, rows1).astype(BF16)
    send_m[...] = mm(eye, spread, NT).astype(BF16).reshape(NY, 16, 128)
    send_y(lambda to: pair_in.at[:, :, to], got_p, 2)
    send_y(lambda to: send_m.at[to], got_m, 3)
    got_p[y] = pair_ref[:, :, y]
    got_m[y] = send_m[y]

    r, s = grid_of(256, 256)
    turn = onehot((r // 16 == s % 16) & ((r // 8) % 2 == (s // 16) % 2) & (r % 8 == s // 32))
    split = onehot((r % 2 == (s // 8) % 2) & ((r // 2) % 16 == s // 16) & (r // 32 == s % 8))
    twice = onehot(lax.broadcasted_iota(jnp.int32, (512, 256), 0) // 2 == lax.broadcasted_iota(jnp.int32, (512, 256), 1))
    even = lax.broadcasted_iota(jnp.int32, (512, 128), 0) % 2 == 0
    gather = onehot((s % 4 == r // 64) & (s // 4 == r % 64))

    arrive(1)
    next_r[...] = mm(split, got_r[...].reshape(256, 256)).astype(BF16).reshape(NY, 32, 256)
    send_y(lambda to: next_r.at[to], have_r, 5)
    arrive(0)
    next_l[...] = mm(turn, got_l[...].reshape(256, 256)).astype(BF16).reshape(NQ, 16, 256)
    send_q(lambda to: next_l.at[to], have_l, 4)
    have_l[q] = next_l[q]
    have_r[y] = next_r[y]

    arrive(2)
    arrive(3)
    m0 = got_m[...].astype(F32)
    m1 = pltpu.roll(m0.reshape(128, 128), 64, 1).reshape(NY, 16, 128)
    m01 = jnp.stack([m0, m1], axis=1).reshape(256, 128).astype(BF16)
    m01 = mm(turn, m01).astype(BF16).reshape(8, 2, 16, 128)
    for z in range(2):
        part = mm(turn, got_p[:, :, z].reshape(256, 128)).astype(BF16)
        next_p[z * 8 : z * 8 + 8, 0:2] = part.reshape(8, 2, 16, 128)
        next_p[z * 8 : z * 8 + 8, 2:4] = m01
    send_q(lambda to: next_p.at[natural(to)], have_p, 6)
    have_p[q] = next_p[natural(q)]

    arrive(5)
    doubled = mm(twice, have_r[...].reshape(256, 256)).astype(BF16)
    arrive(4)
    tri = mm(doubled, have_l[...].reshape(256, 256), NT)
    tri = jnp.where(even, tri[:, :128], tri[:, 128:])
    send_t[...] = tri.reshape(128, 4, 128).astype(BF16)
    sent[7] = due[7] = have_t.at[pl.ds(0, 127)]
    place = y * 16 + q
    for step in FAR_ALL:
        to, part = at_q[step[0], step[2], step[3]]
        send(send_t.at[y_slot[step[1]] + to], have_t.at[place], 7, part + y_part[step[1]])
    have_t[place] = send_t[place]

    arrive(6)
    pairs, gates, lives = [], [], []
    pick = onehot(lane == zl)
    for jj in range(2):
        p = mm(eye, have_p[:, jj].reshape(256, 128), NT)
        zc = norm(p, 0).astype(BF16)
        pairs.append(p)
        gates.append(jax.nn.sigmoid(mm(wg_ref[...], zc, YN)))
        lives.append(mm(have_p[:, 2 + jj].reshape(256, 128), pick))
    wa = wa_ref[...]
    wq_t, wk_t, wv_t, wgate_t, wo_t = (
        mm(eye, w, NT).astype(BF16) for w in (wa[:, :128], wa[:, 128:256], wa[:, 256:384], wa[:, 384:], wo_ref[...])
    )

    order = onehot(
        (s // 128 == (r // 16) % 2)
        & ((s // 16) % 8 == r % 8)
        & ((s // 8) % 2 == r // 128)
        & ((s // 4) % 2 == (r // 8) % 2)
        & (s % 4 == (r // 32) % 4)
    )
    arrive(7)

    p1s, yns = [], []
    tris = [mm(gather, have_t[b * 64 : b * 64 + 64].reshape(256, 128)).reshape(4, 64, 128) for b in range(2)]
    for jj in range(2):
        t = jnp.concatenate(
            [jnp.concatenate([tris[b][jj * 2 + half] for b in range(2)], axis=0) for half in range(2)], axis=1
        )
        tn = norm(t, 0).astype(BF16)
        p1 = pairs[jj] + gates[jj] * mm(wo_t, tn)
        p1s.append(p1)
        yns.append(norm(p1, 0).astype(BF16))

    parts = [mm(wb_ref[...], yn) for yn in yns]
    both = jnp.concatenate(parts, axis=0)
    send_b[...] = jnp.concatenate([both[:, :128], both[:, 128:]], axis=0).astype(BF16)
    chip = q % 8
    for step in sorted(FAR_ALL, key=lambda v: (-(v[0] + 0.6 * min(v[1], 8 - v[1]) + 1.2 * min(v[2], 4 - v[2])), v)):
        if step[3] == 0:
            send(send_b, have_b.at[core, chip, y], 9 + step[1], at_q[step[0], step[2], 0][1] + y_part[step[1]])
    have_b[core, chip, y] = send_b[...]
    for k in range(NY):
        sent[9 + k] = have_b.at[0, pl.ds(0, 8 if k else 7), 0]

    keys, queries, values = [], [], []
    for jj in range(2):
        keys.append(mm(mm(wk_t, yns[jj]).astype(BF16), eye, YN).astype(BF16))
        queries.append(mm(wq_t, yns[jj]).astype(BF16))
        values.append(mm(wv_t, yns[jj]).astype(BF16))
        gate = jax.nn.sigmoid(mm(wgate_t, yns[jj]))
        for half in range(2):
            pair1[jj, half] = p1s[jj][:, half * 128 : half * 128 + 128].T
            out_gates[jj, half] = gate[:, half * 128 : half * 128 + 128]

    head_row = lax.broadcasted_iota(jnp.int32, (128, 256), 0) // 32
    scale = F32(32.0**-0.5)
    for jj in range(2):
        for h in range(4):
            qh = jnp.where(head_row == h, queries[jj].astype(F32), F32(0)).astype(BF16)
            score = mm(keys[jj], qh) * scale
            for half in range(2):
                scores[jj, h, half] = score[:, half * 128 : half * 128 + 128]

    sent[17] = due[17] = have_b.at[0]
    for k in (0, 1, 7, 2, 6, 3, 5, 4):
        wait_on(sent[9 + k], rsem.at[9 + k])
        block = have_b.at[core, :, (y + NY - k) % NY]
        send(block, block, 17, near)

    ones = jnp.ones((16, 256), BF16)

    def finish(half):
        biases = [
            mm(order, have_b[half, 2 * b : 2 * b + 2].reshape(256, 128)).astype(BF16).reshape(8, 32, 128) for b in range(4)
        ]
        atts = [[], []]
        for h in range(4):
            bias = jnp.concatenate(
                [mm(eye, jnp.concatenate([b[kh * 4 + h] for b in biases], axis=0), NT) for kh in range(2)], axis=0
            )
            for jj in range(2):
                sc = jnp.where(lives[jj] > 0.5, scores[jj, h, half] + bias, F32(-1e9))
                e = jnp.exp(sc - jnp.max(sc, axis=0, keepdims=True))
                o = mm(jnp.concatenate([values[jj][h * 32 : (h + 1) * 32], ones], axis=0), e.astype(BF16))
                atts[jj].append(o[:32] / o[32:33])
        for jj in range(2):
            att = (jnp.concatenate(atts[jj], axis=0) * out_gates[jj, half]).astype(BF16)
            res = pair1[jj, half] + mm(att, wao_ref[...], YN)
            for k in range(8):
                for ii in range(2):
                    start = (k // 4) * 256 + (k % 4 * 2 + half) * 4 + ii * 2 + jj
                    out_ref[pl.ds(start, 8, stride=32), :] = res[k * 16 + ii * 8 : k * 16 + ii * 8 + 8]

    finish(core)
    arrive(17)
    finish(1 - core)

    for k, ref in sent.items():
        wait_on(ref, ssem.at[k])


def shards(pair, pair_mask, wl, wr, wg, wo, wa, wb, wao):
    vm = pl.BlockSpec(memory_space=pltpu.VMEM)
    hbm = pl.BlockSpec(memory_space=pltpu.HBM)
    inputs = (pair.reshape(2, 2, 8, 16, 128), pair_mask, wl, wr, wg, wo, wa, wb.T, wao)
    out = pl.pallas_call(
        kernel,
        out_shape=jax.ShapeDtypeStruct((512, 128), F32),
        in_specs=[hbm] * 9,
        out_specs=vm,
        scratch_shapes=[
            pltpu.VMEM((2, 2, 8, 16, 128), BF16),
            pltpu.VMEM((2, 256), jnp.int32),
            pltpu.VMEM((128, 256), BF16),
            pltpu.VMEM((128, 256), BF16),
            pltpu.VMEM((128, 128), BF16),
            pltpu.VMEM((128, 128), BF16),
            pltpu.VMEM((128, 512), BF16),
            pltpu.VMEM((4, 128), BF16),
            pltpu.VMEM((128, 128), BF16),
            pltpu.VMEM((NY, 2, 16, 256), BF16),
            pltpu.VMEM((NQ, 16, 256), BF16),
            pltpu.VMEM((NY, 16, 128), BF16),
            pltpu.VMEM((NY, 2, 16, 256), BF16),
            pltpu.VMEM((NQ, 16, 256), BF16),
            pltpu.VMEM((NY, 2, 2, 16, 128), BF16),
            pltpu.VMEM((NY, 16, 128), BF16),
            pltpu.VMEM((NQ, 16, 256), BF16),
            pltpu.VMEM((NY, 32, 256), BF16),
            pltpu.VMEM((NQ, 4, 16, 128), BF16),
            pltpu.VMEM((NQ, 16, 256), BF16),
            pltpu.VMEM((NY, 32, 256), BF16),
            pltpu.VMEM((NQ, 4, 16, 128), BF16),
            pltpu.VMEM((128, 4, 128), BF16),
            pltpu.VMEM((128, 4, 128), BF16),
            pltpu.VMEM((16, 128), BF16),
            pltpu.VMEM((2, 8, NY, 16, 128), BF16),
            pltpu.VMEM((2, 4, 2, 256, 128), F32),
            pltpu.VMEM((2, 2, 128, 128), F32),
            pltpu.VMEM((2, 2, 128, 128), F32),
            pltpu.SemaphoreType.DMA((18,)),
            pltpu.SemaphoreType.DMA((18,)),
            pltpu.SemaphoreType.DMA((9,)),
        ],
        compiler_params=pltpu.CompilerParams(
            collective_id=0, has_side_effects=True, vmem_limit_bytes=32 * 1024 * 1024
        ),
    )(*(pltpu.with_memory_space_constraint(a, pltpu.HBM) for a in inputs))
    return out.reshape(256, 2, 128)


def solution(mesh):
    rows = ("dp", "dap")
    return jax.shard_map(
        shards,
        mesh=mesh,
        in_specs=(P(rows, None, None), P(rows, None), P(), P(), P(), P(), P(), P(), P()),
        out_specs=P("dp", "dap", None),
        check_vma=False,
    )
```
